32 devices in a mesh: st: 2 (over x), fsdp: 16 (over z, y, core).
Axes of the slice: x: 2, y: 2, z: 4, core: 2. Of those that a mesh axis runs over, the one named last changes fastest.
Arguments:
- normed: bfloat16 [16, 512, 3072], P('fsdp')
- qkv_weight: bfloat16 [3072, 8, 384], P('fsdp', 'st'), may hold values from -0.109375 to 0.109375
- out_weight: bfloat16 [3072, 1024], P('fsdp', 'st'), may hold values from -0.1875 to 0.1875
- segment_ids: int32 [16], replicated, may hold values from 0 to 3, never falling along the last dimension, each value on 1 to 8 neighbouring positions
Outputs:
- attended: bfloat16 [16, 512, 3072], P('fsdp', 'st')
The draws below stay inside these ranges and needn't reach their ends.
Inputs may be any that keep to these rules, and one draw needn't show every extreme that they name: `segment_ids`: segment ids never fall from one frame to the next; each clip covers 1 to 8 consecutive frames, and one covers exactly 8.
All inputs are finite; a program needn't handle non-finite values.
Results may differ from the reference program's by a relative error of at most 0.017.
Values may be sent and summed in bfloat16 or wider, within the bound.
No kernel may reach another device: no remote copies, remote signals or barrier semaphores. Data moves between devices by JAX's collectives and lax.ppermute only.
A program may use at most 64 MiB of HBM per device.

```python
import math
import jax
import jax.numpy as jnp
import numpy as np
from jax import lax

D = 3072
HEAD = 128
HS_DEV = 2
HT_DEV = 2
P_SIZE = 512
CLIP = 8
HEADS = 8
FRAMES = 16
SEGS = 4
N_ST = 2


def draw_normed(key, part):
    first = jax.random.fold_in(key, 0)
    return jax.random.normal(first, (FRAMES, P_SIZE, D), jnp.float32).astype(jnp.bfloat16)


def block_scale(stream_key, dims, pieces, least, top_value):
    loudness = 1.0
    for axis_at, parts in pieces:
        draws = jax.random.uniform(jax.random.fold_in(jax.random.fold_in(stream_key, 6), axis_at), (parts,), jnp.float32, least / len(pieces), top_value / len(pieces))
        loudness = loudness * jnp.repeat(jnp.exp(draws), dims[axis_at] // parts).reshape((-1,) + (1,) * (len(dims) - 1 - axis_at))
    return loudness


def profile(amount, total, bound, lean):
    loads = [(1 << 20) // math.isqrt(standing ** lean) + 1 for standing in range(2, amount + 1)]
    rest, counts = total - bound - (amount - 1), [1] * (amount - 1)
    while rest > 0:
        movable = [i for i in range(amount - 1) if counts[i] < bound]
        mass, left = sum([loads[i] for i in movable]), rest
        for i in movable:
            addition = min(bound - counts[i], max(1, left * loads[i] // mass), rest)
            counts[i] = counts[i] + addition
            rest = rest - addition
    return np.array([bound] + counts)


def uneven(key, count, total, reach, skew):
    if count == 2:
        one = jax.random.randint(key, (), max(1, total - reach), min(reach, total - 1) + 1)
        return jnp.stack([one, total - one])
    sizes = jnp.asarray(profile(count, total, reach, skew), jnp.int32)
    couples = (count - 1) // 2
    giver, sink = sizes[1:1 + 2 * couples:2], sizes[2:2 + 2 * couples:2]
    margin = jnp.minimum(giver - 1, reach - sink)
    moved = jax.random.randint(jax.random.fold_in(key, 1), (couples,), 0, 1 << 20) % (margin + 1)
    sizes = sizes.at[1:1 + 2 * couples:2].set(giver - moved).at[2:2 + 2 * couples:2].set(sink + moved)
    return sizes[jax.random.permutation(jax.random.fold_in(key, 2), count)]


def normal_values(rng, dims, scale, most, cuts=(), kind=jnp.bfloat16):
    loudness = block_scale(rng, dims, cuts, -0.22, 0.18) if cuts else 1.0
    array = jax.random.normal(rng, dims, jnp.float32) * scale * loudness
    return jnp.minimum(jnp.maximum(array, -most), most).astype(kind)


def setup_inputs(seed: int = 0) -> dict:
    seeds = jax.random.split(jax.random.key(seed), 5)
    normed = draw_normed(jax.random.fold_in(seeds[4], 71), 0)
    qkv_weight = normal_values(seeds[1], (D, HEADS, 3 * HEAD), D ** -0.5, 0.109375, ((0, 16), (1, 2)))
    out_weight = normal_values(seeds[2], (D, HEADS * HEAD), (HEADS * HEAD) ** -0.5, 0.1875, ((0, 16), (1, 2)))
    segment_ids = jnp.searchsorted(jnp.cumsum(uneven(seeds[3], SEGS, FRAMES, CLIP, 0)), jnp.arange(FRAMES), side="right").astype(jnp.int32)
    return dict(normed=normed, qkv_weight=qkv_weight, out_weight=out_weight, segment_ids=segment_ids)


def softmax_rows(scores):
    top = lax.optimization_barrier(jnp.max(scores, axis=-1, keepdims=True))
    expo = jnp.exp(scores - top)
    return expo / lax.optimization_barrier(jnp.sum(expo, axis=-1, keepdims=True))

def reference(normed, qkv_weight, out_weight, segment_ids):
    group = HS_DEV + HT_DEV
    scale = 1.0 / math.sqrt(HEAD)
    weight_flat = qkv_weight.reshape(D, HEADS * 3 * HEAD)

    def frame_work(frame):
        packed = jnp.dot(frame, weight_flat, preferred_element_type=jnp.float32).astype(jnp.bfloat16)
        packed = packed.reshape(P_SIZE, N_ST, group, 3 * HEAD)
        spatial = packed[:, :, :HS_DEV].reshape(P_SIZE, N_ST * HS_DEV, 3 * HEAD).astype(jnp.float32)
        query = spatial[..., :HEAD]
        keys = spatial[..., HEAD:2 * HEAD]
        values = spatial[..., 2 * HEAD:]
        scores = jnp.einsum('qhc,khc->hqk', query, keys) * scale
        weights = softmax_rows(scores).astype(jnp.bfloat16).astype(jnp.float32)
        spatial_out = jnp.einsum('hqk,khc->qhc', weights, values).astype(jnp.bfloat16)
        return (spatial_out.reshape(P_SIZE, N_ST, HS_DEV, HEAD), packed[:, :, HS_DEV:])
    spatial_out, temporal = lax.map(frame_work, normed)
    temporal = temporal.astype(jnp.float32)
    query = temporal[..., :HEAD]
    keys = temporal[..., HEAD:2 * HEAD]
    values = temporal[..., 2 * HEAD:]
    scores = jnp.einsum('tpshc,upshc->pshtu', query, keys) * scale
    same = segment_ids[:, None] == segment_ids[None, :]
    scores = jnp.where(same, scores, jnp.float32(-1e+30))
    weights = softmax_rows(scores).astype(jnp.bfloat16).astype(jnp.float32)
    temporal_out = jnp.einsum('pshtu,upshc->tpshc', weights, values).astype(jnp.bfloat16)
    heads_out = jnp.concatenate([spatial_out, temporal_out], axis=3)
    heads_out = heads_out.reshape(FRAMES * P_SIZE, N_ST, group * HEAD)
    out_groups = out_weight.reshape(D, N_ST, group * HEAD)
    total = jnp.zeros((FRAMES * P_SIZE, D), jnp.float32)
    for index in range(N_ST):
        partial_sum = lax.dot_general(heads_out[:, index], out_groups[:, index], (((1,), (1,)), ((), ())), preferred_element_type=jnp.float32)
        total = total + partial_sum.astype(jnp.bfloat16).astype(jnp.float32)
    return total.astype(jnp.bfloat16).reshape(FRAMES, P_SIZE, D)
```

```python
import functools
import math

import jax
import jax.numpy as jnp
from jax import lax
from jax.experimental import pallas as pl
from jax.experimental.pallas import tpu as pltpu
from jax.sharding import PartitionSpec as P

HEAD = 128
HS_DEV = 2
SCALE = 1.0 / math.sqrt(HEAD)
VMEM_LIMIT = 40 * 1024 * 1024


def vmem_call(body, out_shape, args, flops, name):
    bytes_moved = sum(a.size * a.dtype.itemsize for a in args)
    return pl.pallas_call(
        body,
        out_shape=out_shape,
        in_specs=[
            pl.BlockSpec(memory_space=pltpu.SMEM if a.dtype == jnp.int32 else pltpu.VMEM)
            for a in args
        ],
        out_specs=pl.BlockSpec(memory_space=pltpu.VMEM),
        compiler_params=pltpu.CompilerParams(vmem_limit_bytes=VMEM_LIMIT),
        cost_estimate=pl.CostEstimate(flops=flops, bytes_accessed=bytes_moved, transcendentals=0),
        name=name,
    )(*args)


def spatial_body(qkv_ref, out_ref):
    patches = qkv_ref.shape[0] // 2
    for frame in range(2):
        rows = pl.ds(frame * patches, patches)
        query = qkv_ref[rows, :HEAD]
        keys = qkv_ref[rows, HEAD : 2 * HEAD]
        values = qkv_ref[rows, 2 * HEAD :]
        scores = lax.dot_general(
            query, keys, (((1,), (1,)), ((), ())), preferred_element_type=jnp.float32
        )
        scores = scores * SCALE
        expo = jnp.exp(scores - jnp.max(scores, axis=-1, keepdims=True))
        total = jnp.sum(expo, axis=-1, keepdims=True)
        result = jnp.dot(expo.astype(jnp.bfloat16), values, preferred_element_type=jnp.float32)
        out_ref[rows, :] = (result / total).astype(jnp.bfloat16)


def temporal_body(tile, meta_ref, qkv_ref, out_ref):
    frames, rows = qkv_ref.shape[0], qkv_ref.shape[1]
    flip = meta_ref[frames]
    size = frames * tile
    row_at = lax.broadcasted_iota(jnp.int32, (size, size), 0)
    col_at = lax.broadcasted_iota(jnp.int32, (size, size), 1)
    row_seg = jnp.zeros((size, 1), jnp.int32)
    col_seg = jnp.zeros((1, size), jnp.int32)
    row_frame = lax.broadcasted_iota(jnp.int32, (size, 1), 0) // tile
    col_frame = lax.broadcasted_iota(jnp.int32, (1, size), 1) // tile
    for frame in range(frames):
        clip = meta_ref[frame]
        row_seg = jnp.where(row_frame == frame, clip, row_seg)
        col_seg = jnp.where(col_frame == frame, clip, col_seg)
    keep = (row_at % tile == col_at % tile) & (row_seg == col_seg)
    for start in range(0, rows, tile):
        block = qkv_ref[:, start : start + tile, :].reshape(size, 3 * HEAD)
        scores = lax.dot_general(
            block[:, :HEAD],
            block[:, HEAD : 2 * HEAD],
            (((1,), (1,)), ((), ())),
            preferred_element_type=jnp.float32,
        )
        scores = jnp.where(keep, scores * SCALE, jnp.float32(-1e30))
        expo = jnp.exp(scores - jnp.max(scores, axis=-1, keepdims=True))
        total = jnp.sum(expo, axis=-1, keepdims=True)
        result = jnp.dot(
            expo.astype(jnp.bfloat16), block[:, 2 * HEAD :], preferred_element_type=jnp.float32
        )
        result = (result / total).astype(jnp.bfloat16).reshape(frames, tile, HEAD)
        for pair in range(frames // 2):
            out_ref[2 * pair + flip, start : start + tile, :] = result[2 * pair]
            out_ref[2 * pair + 1 - flip, start : start + tile, :] = result[2 * pair + 1]


def shards(n_st, n_fsdp, normed, qkv_weight, out_weight, segment_ids):
    patches, width = normed.shape[1], normed.shape[2]
    frames = n_fsdp
    depth = qkv_weight.shape[0]
    chips = n_fsdp // 2
    ring = list(range(0, chips, 2)) + list(range(chips - 1, 0, -2))
    place = [ring.index(chip) for chip in range(chips)]
    me = lax.axis_index("fsdp")
    st = lax.axis_index("st")
    chip, core = me // 2, me % 2
    spot = jnp.array(place, jnp.int32)[chip]
    ring_table = jnp.array(ring, jnp.int32)

    swap = [(i, i ^ 1) for i in range(n_fsdp)]
    forward = [
        (2 * ring[i] + c, 2 * ring[(i + 1) % chips] + c) for i in range(chips) for c in range(2)
    ]
    backward = [(b, a) for a, b in forward]

    def to_core(x):
        return lax.ppermute(x, "fsdp", swap)

    def by_core(mine, other, axis):
        return jnp.where(
            core == 0,
            jnp.concatenate([mine, other], axis=axis),
            jnp.concatenate([other, mine], axis=axis),
        )

    def st_exchange(x):
        if n_st != 2:
            return lax.all_to_all(x, "st", split_axis=0, concat_axis=0, tiled=True)
        mine = lax.dynamic_slice_in_dim(x, st, 1, 0)
        other = lax.dynamic_slice_in_dim(x, 1 - st, 1, 0)
        other = lax.ppermute(other, "st", [(0, 1), (1, 0)])
        return jnp.where(
            st == 0, jnp.concatenate([mine, other]), jnp.concatenate([other, mine])
        )

    def st_gather(x):
        if n_st != 2:
            return lax.all_gather(x, "st", axis=1, tiled=True)
        other = lax.ppermute(x, "st", [(0, 1), (1, 0)])
        return jnp.where(
            st == 0,
            jnp.concatenate([x, other], axis=1),
            jnp.concatenate([other, x], axis=1),
        )

    def ring_gather(piece):
        groups = [[piece]]
        ahead = behind = piece
        for _ in range(chips // 2 - 1):
            ahead = lax.ppermute(ahead, "fsdp", forward)
            behind = lax.ppermute(behind, "fsdp", backward)
            groups.append([ahead, behind])
        half = piece.shape[0] // 2
        ahead = lax.ppermute(ahead[:half], "fsdp", forward)
        behind = lax.ppermute(behind[half:], "fsdp", backward)
        groups.append([jnp.concatenate([ahead, behind])])
        return groups

    offsets = [0]
    for d in range(1, chips // 2):
        offsets += [chips - d, d]
    offsets.append(chips // 2)
    sources = [ring_table[(spot + d) % chips] for d in offsets]

    def take_head(first):
        mine = lax.dynamic_slice_in_dim(qkv_weight, first + core, 1, 1)[:, 0]
        other = lax.dynamic_slice_in_dim(qkv_weight, first + 1 - core, 1, 1)[:, 0]
        return by_core(mine, to_core(other), 1)

    temporal_piece = take_head(HS_DEV)
    own = normed.reshape(patches, width)
    rows = jnp.concatenate([own, to_core(own)])
    spatial_piece = take_head(0)
    chip_width = 2 * depth
    rows = jnp.concatenate(
        [lax.dynamic_slice_in_dim(rows, s * chip_width, chip_width, 1) for s in sources], axis=1
    )

    def project(pieces):
        weight = jnp.concatenate(
            [p[:, k * 3 * HEAD : (k + 1) * 3 * HEAD] for p in pieces for k in range(2)]
        )
        return jnp.dot(rows, weight, preferred_element_type=jnp.float32).astype(jnp.bfloat16)

    groups = ring_gather(temporal_piece)
    temporal = project([p for g in groups for p in g])
    part = patches // (n_st * chips)
    temporal = temporal.reshape(2, n_st, chips, part, 3 * HEAD).transpose(2, 0, 1, 3, 4)
    same_core = [[2 * i + c for i in range(chips)] for c in range(2)]
    temporal = lax.all_to_all(
        temporal,
        "fsdp",
        split_axis=0,
        concat_axis=0,
        tiled=True,
        axis_index_groups=same_core,
    ).reshape(frames, n_st * part, 3 * HEAD)
    pairs = segment_ids.reshape(chips, 2)
    pairs = jnp.where(core == 0, pairs, pairs[:, ::-1]).reshape(frames)
    meta = jnp.concatenate([pairs, core.reshape(1)]).astype(jnp.int32)
    tile = max(1, 256 // frames)
    tile = min(n_st * part, max(16, tile))
    result = vmem_call(
        functools.partial(temporal_body, tile),
        jax.ShapeDtypeStruct((frames, n_st * part, HEAD), jnp.bfloat16),
        [meta, temporal],
        4 * frames * frames * n_st * part * tile * HEAD,
        "temporal_attention",
    )
    result = result.reshape(frames, n_st, part, HEAD).transpose(1, 0, 2, 3)
    result = lax.all_to_all(
        result.reshape(n_st * frames, part, HEAD),
        ("st", "fsdp"),
        split_axis=0,
        concat_axis=0,
        tiled=True,
    )
    result = result.reshape(n_st, chips, 2, part, HEAD).transpose(1, 3, 0, 2, 4)
    temporal_heads = result.reshape(patches // n_st, n_st, 2, HEAD)

    groups = ring_gather(jnp.concatenate([spatial_piece, out_weight], axis=1))
    split = spatial_piece.shape[1]
    out_pieces = [
        st_gather(jnp.concatenate([p[:, split:] for p in g]) if len(g) > 1 else g[0][:, split:])
        for g in groups
    ]
    out_mine = jnp.concatenate(out_pieces)
    out_other = to_core(out_mine)
    spatial = project([p[:, :split] for g in groups for p in g])
    spatial = vmem_call(
        spatial_body,
        jax.ShapeDtypeStruct((2 * patches, HEAD), jnp.bfloat16),
        [spatial],
        8 * patches * patches * HEAD,
        "spatial_attention",
    )
    spatial = spatial.reshape(2, n_st, patches // n_st, HEAD).transpose(1, 0, 2, 3)
    spatial = st_exchange(spatial)
    mine, other = spatial[:, 0], to_core(spatial[:, 1])
    spatial_heads = by_core(mine[:, :, None], other[:, :, None], 2).transpose(1, 0, 2, 3)

    heads = jnp.concatenate([spatial_heads, temporal_heads], axis=2)
    heads = heads.reshape(patches // n_st, n_st * 4 * HEAD)
    out_all = by_core(
        out_mine.reshape(chips, 1, depth, -1), out_other.reshape(chips, 1, depth, -1), 1
    )
    out_all = out_all.reshape(width, -1)
    attended = lax.dot_general(
        heads, out_all, (((1,), (1,)), ((), ())), preferred_element_type=jnp.float32
    ).astype(jnp.bfloat16)
    home = [offsets.index(d) for d in range(chips)]
    home_table = jnp.array(home, jnp.int32)
    place_table = jnp.array(place, jnp.int32)
    blocks = []
    for q in range(chips):
        at = home_table[(place_table[q] - spot + chips) % chips]
        blocks.append(lax.dynamic_slice_in_dim(attended, at * chip_width, chip_width, 1))
    attended = jnp.concatenate(blocks, axis=1)
    return attended.reshape(1, patches // n_st, width)


def solution(mesh):
    return jax.shard_map(
        functools.partial(shards, mesh.shape["st"], mesh.shape["fsdp"]),
        mesh=mesh,
        in_specs=(P("fsdp", None, None), P("fsdp", "st", None), P("fsdp", "st"), P()),
        out_specs=P("fsdp", "st", None),
        check_vma=False,
    )
```

```python
import functools
import math

import jax
import jax.numpy as jnp
from jax import lax
from jax.experimental import pallas as pl
from jax.experimental.pallas import tpu as pltpu
from jax.sharding import PartitionSpec as P

HEAD = 128
HS_DEV = 2
SCALE = 1.0 / math.sqrt(HEAD)
VMEM_LIMIT = 32 * 1024 * 1024


def vmem_call(body, out_shape, args, flops, name, scratch=()):
    bytes_moved = sum(a.size * a.dtype.itemsize for a in args)
    return pl.pallas_call(
        body,
        out_shape=out_shape,
        in_specs=[
            pl.BlockSpec(memory_space=pltpu.SMEM if a.dtype == jnp.int32 else pltpu.VMEM)
            for a in args
        ],
        out_specs=pl.BlockSpec(memory_space=pltpu.VMEM),
        scratch_shapes=list(scratch),
        compiler_params=pltpu.CompilerParams(vmem_limit_bytes=VMEM_LIMIT),
        cost_estimate=pl.CostEstimate(flops=flops, bytes_accessed=bytes_moved, transcendentals=0),
        name=name,
    )(*args)


def place_weight(meta_ref, piece_refs, weight):
    depth = piece_refs[0].shape[0]
    core = meta_ref[0]
    columns = weight.shape[1]
    slot, first = 0, 0
    for ref in piece_refs:
        rows = ref.shape[0]
        chip = meta_ref[2 + slot]
        for k in range(2):
            at = (chip * 2 + (core if k == 0 else 1 - core)) * depth + first
            weight[pl.ds(pl.multiple_of(at, 16), rows), :] = ref[
                :, k * columns : (k + 1) * columns
            ]
        first += rows
        if first == depth:
            slot, first = slot + 1, 0


def project_body(chips, n_st, direct, meta_ref, own_ref, other_ref, *refs):
    *piece_refs, out_ref, weight = refs
    place_weight(meta_ref, piece_refs, weight)
    patches = own_ref.shape[0]
    part = patches // (n_st * chips)
    half = patches // 2
    for frame, ref in enumerate((own_ref, other_ref)):
        for first in range(0, patches, half):
            result = jnp.dot(
                ref[first : first + half, :], weight[...], preferred_element_type=jnp.float32
            ).astype(jnp.bfloat16)
            if not direct:
                out_ref[frame * patches + first : frame * patches + first + half, :] = result
                continue
            for at in range(first, first + half, part):
                block = at // part
                out_ref[block % chips, frame, block // chips] = result[
                    at - first : at - first + part
                ]


def spatial_body(n_st, meta_ref, own_ref, other_ref, *refs):
    *piece_refs, out_ref, weight, packed = refs
    place_weight(meta_ref, piece_refs, weight)
    patches = own_ref.shape[0]
    part = patches // n_st
    half = patches // 2
    for frame, ref in enumerate((own_ref, other_ref)):
        for first in range(0, patches, half):
            packed[first : first + half, :] = jnp.dot(
                ref[first : first + half, :], weight[...], preferred_element_type=jnp.float32
            ).astype(jnp.bfloat16)
        for group in range(n_st):
            rows = slice(group * part, (group + 1) * part)
            scores = lax.dot_general(
                packed[rows, :HEAD],
                packed[:, HEAD : 2 * HEAD],
                (((1,), (1,)), ((), ())),
                preferred_element_type=jnp.float32,
            )
            scores = scores * SCALE
            expo = jnp.exp(scores - jnp.max(scores, axis=-1, keepdims=True))
            total = jnp.sum(expo, axis=-1, keepdims=True)
            result = jnp.dot(
                expo.astype(jnp.bfloat16),
                packed[:, 2 * HEAD :],
                preferred_element_type=jnp.float32,
            )
            result = (result / total).astype(jnp.bfloat16)
            place = (group + meta_ref[1]) % 2 if n_st == 2 else group
            out_ref[place, frame] = result


def temporal_body(tile, meta_ref, qkv_ref, out_ref):
    frames, rows = qkv_ref.shape[0], qkv_ref.shape[1]
    part = out_ref.shape[2]
    flip = meta_ref[frames]
    size = frames * tile
    row_at = lax.broadcasted_iota(jnp.int32, (size, size), 0)
    col_at = lax.broadcasted_iota(jnp.int32, (size, size), 1)
    row_seg = jnp.zeros((size, 1), jnp.int32)
    col_seg = jnp.zeros((1, size), jnp.int32)
    row_frame = lax.broadcasted_iota(jnp.int32, (size, 1), 0) // tile
    col_frame = lax.broadcasted_iota(jnp.int32, (1, size), 1) // tile
    for frame in range(frames):
        clip = meta_ref[frame]
        row_seg = jnp.where(row_frame == frame, clip, row_seg)
        col_seg = jnp.where(col_frame == frame, clip, col_seg)
    keep = (row_at % tile == col_at % tile) & (row_seg == col_seg)
    for start in range(0, rows, tile):
        block = qkv_ref[:, start : start + tile, :].reshape(size, 3 * HEAD)
        scores = lax.dot_general(
            block[:, :HEAD],
            block[:, HEAD : 2 * HEAD],
            (((1,), (1,)), ((), ())),
            preferred_element_type=jnp.float32,
        )
        scores = jnp.where(keep, scores * SCALE, jnp.float32(-1e30))
        expo = jnp.exp(scores - jnp.max(scores, axis=-1, keepdims=True))
        total = jnp.sum(expo, axis=-1, keepdims=True)
        result = jnp.dot(
            expo.astype(jnp.bfloat16), block[:, 2 * HEAD :], preferred_element_type=jnp.float32
        )
        result = (result / total).astype(jnp.bfloat16).reshape(frames, tile, HEAD)
        for pair in range(frames // 2):
            for k in range(2):
                at = 2 * pair + (flip if k == 0 else 1 - flip)
                if part % tile:
                    out_ref[0, at, start : start + tile, :] = result[2 * pair + k]
                else:
                    low = start % part
                    out_ref[start // part, at, low : low + tile, :] = result[2 * pair + k]


def place_out_body(depth, meta_ref, *refs):
    *piece_refs, weight = refs
    core, st = meta_ref[0], meta_ref[1]
    columns = piece_refs[0].shape[1]
    count = len(piece_refs) // 4
    for kind in range(4):
        group = st if kind < 2 else 1 - st
        side = core if kind % 2 == 0 else 1 - core
        slot = 0
        for ref in piece_refs[kind * count : (kind + 1) * count]:
            for first in range(0, ref.shape[0], depth):
                at = (meta_ref[2 + slot] * 2 + side) * depth
                weight[
                    pl.ds(pl.multiple_of(at, 16), depth),
                    pl.ds(pl.multiple_of(group * columns, 128), columns),
                ] = ref[first : first + depth, :]
                slot += 1


def out_body(meta_ref, mine_ref, peer_ref, core_ref, temporal_ref, weight_ref, out_ref, heads):
    core, st = meta_ref[0], meta_ref[1]
    n_st, chips, _, part, _ = temporal_ref.shape
    group = heads.shape[1] // n_st

    def columns(which, head):
        return pl.ds(pl.multiple_of(which * group + head * HEAD, 128), HEAD)

    heads[:, columns(st, core)] = mine_ref[0]
    heads[:, columns(1 - st, core)] = peer_ref[0]
    heads[:, columns(st, 1 - core)] = core_ref[0]
    heads[:, columns(1 - st, 1 - core)] = core_ref[1]
    for which in range(n_st):
        for chip in range(chips):
            for k in range(2):
                heads[
                    chip * part : (chip + 1) * part,
                    which * group + (HS_DEV + k) * HEAD : which * group + (HS_DEV + k + 1) * HEAD,
                ] = temporal_ref[which, chip, k]
    width = weight_ref.shape[0]
    step = 768 if width % 768 == 0 else width
    for at in range(0, width, step):
        out_ref[:, at : at + step] = lax.dot_general(
            heads[...],
            weight_ref[at : at + step, :],
            (((1,), (1,)), ((), ())),
            preferred_element_type=jnp.float32,
        ).astype(jnp.bfloat16)


def shards(n_st, n_fsdp, normed, qkv_weight, out_weight, segment_ids):
    patches, width = normed.shape[1], normed.shape[2]
    frames = n_fsdp
    depth = qkv_weight.shape[0]
    chips = n_fsdp // 2
    part = patches // (n_st * chips)
    rows = patches // n_st
    direct = part % 16 == 0
    ring = list(range(0, chips, 2)) + list(range(chips - 1, 0, -2))
    place = [ring.index(chip) for chip in range(chips)]
    me = lax.axis_index("fsdp")
    st = lax.axis_index("st")
    chip, core = me // 2, me % 2
    spot = jnp.array(place, jnp.int32)[chip]

    swap = [(i, i ^ 1) for i in range(n_fsdp)]
    forward = [
        (2 * ring[i] + c, 2 * ring[(i + 1) % chips] + c) for i in range(chips) for c in range(2)
    ]
    backward = [(b, a) for a, b in forward]

    def to_core(x):
        return lax.ppermute(x, "fsdp", swap)

    def to_peer(x):
        return lax.ppermute(x, "st", [(0, 1), (1, 0)])

    def ring_gather(piece, after=None):
        groups = [[piece]]
        ahead = behind = piece
        for _ in range(chips // 2 - 1):
            ahead = lax.ppermute(ahead, "fsdp", forward)
            behind = lax.ppermute(behind, "fsdp", backward)
            groups.append([ahead, behind])
        half = piece.shape[0] // 2
        ahead = lax.ppermute(ahead[:half], "fsdp", forward)
        behind = lax.ppermute(behind[half:], "fsdp", backward)
        groups.append([ahead, behind])
        return groups

    def pieces_of(groups, columns):
        pieces = [p[:, columns] for g in groups[:-1] for p in g]
        last = [p[:, columns] for p in groups[-1]]
        if last[0].shape[0] % 16:
            last = [jnp.concatenate(last)]
        return pieces + last

    offsets = [0]
    for d in range(1, chips // 2):
        offsets += [chips - d, d]
    offsets.append(chips // 2)
    sources = jnp.array(ring, jnp.int32)[(spot + jnp.array(offsets, jnp.int32)) % chips]
    meta = jnp.concatenate([core.reshape(1), st.reshape(1), sources]).astype(jnp.int32)

    by_head = qkv_weight.transpose(1, 0, 2)

    def take_head(heads):
        mine = lax.dynamic_index_in_dim(heads, core, 0, keepdims=False)
        other = lax.dynamic_index_in_dim(heads, 1 - core, 0, keepdims=False)
        return jnp.concatenate([mine, to_core(other)], axis=1)

    temporal_piece = take_head(lax.optimization_barrier(by_head[HS_DEV:]))
    own = normed.reshape(patches, width)

    groups = ring_gather(temporal_piece)
    first_step = groups[1]
    own, later_head, later_out, _ = lax.optimization_barrier(
        (own, by_head[:HS_DEV], out_weight, temporal_piece)
    )
    other = to_core(own)
    spatial_piece = take_head(later_head)
    head_flops = 4 * patches * width * 3 * HEAD
    weight_scratch = pltpu.VMEM((width, 3 * HEAD), jnp.bfloat16)
    shape = (chips, 2, n_st, part, 3 * HEAD) if direct else (2 * patches, 3 * HEAD)
    temporal = vmem_call(
        functools.partial(project_body, chips, n_st, direct),
        jax.ShapeDtypeStruct(shape, jnp.bfloat16),
        [meta, own, other, *pieces_of(groups, slice(None))],
        head_flops,
        "temporal_projection",
        [weight_scratch],
    )
    if not direct:
        temporal = temporal.reshape(2, n_st, chips, part, 3 * HEAD).transpose(2, 0, 1, 3, 4)
    same_core = [[2 * i + c for i in range(chips)] for c in range(2)]
    temporal = lax.all_to_all(
        temporal,
        "fsdp",
        split_axis=0,
        concat_axis=0,
        tiled=True,
        axis_index_groups=same_core,
    ).reshape(frames, n_st * part, 3 * HEAD)
    pairs = segment_ids.reshape(chips, 2)
    pairs = jnp.where(core == 0, pairs, pairs[:, ::-1]).reshape(frames)
    clips = jnp.concatenate([pairs, core.reshape(1)]).astype(jnp.int32)
    tile = min(n_st * part, max(16, 256 // frames))
    if part % tile == 0:
        shape = (n_st, frames, part, HEAD)
    else:
        shape = (1, frames, n_st * part, HEAD)
    result = vmem_call(
        functools.partial(temporal_body, tile),
        jax.ShapeDtypeStruct(shape, jnp.bfloat16),
        [clips, temporal],
        4 * frames * frames * n_st * part * tile * HEAD,
        "temporal_attention",
    )
    if part % tile:
        result = result.reshape(frames, n_st, part, HEAD).transpose(1, 0, 2, 3)
    result = lax.all_to_all(
        result.reshape(n_st * frames, part, HEAD),
        ("st", "fsdp"),
        split_axis=0,
        concat_axis=0,
        tiled=True,
    )
    temporal_heads = result.reshape(n_st, chips, 2, part, HEAD)

    split = spatial_piece.shape[1]
    both = jnp.concatenate([spatial_piece, later_out], axis=1)
    both, _ = lax.optimization_barrier((both, groups[-2]))
    groups = ring_gather(both)
    spatial = vmem_call(
        functools.partial(spatial_body, n_st),
        jax.ShapeDtypeStruct((n_st, 2, rows, HEAD), jnp.bfloat16),
        [meta, own, other, *pieces_of(groups, slice(0, split))],
        head_flops + 8 * patches * patches * HEAD,
        "spatial_heads",
        [weight_scratch, pltpu.VMEM((patches, 3 * HEAD), jnp.bfloat16)],
    )
    out_groups = [jnp.concatenate([p[:, split:] for p in g]) for g in groups]

    if n_st == 2 and direct:
        peer = to_peer(spatial[1])
        core_heads = to_core(jnp.stack([spatial[0, 1], peer[1]]))
        peer_groups = [to_peer(g) for g in out_groups]
        mine_all, peer_all = jnp.concatenate(out_groups), jnp.concatenate(peer_groups)
        weight = vmem_call(
            functools.partial(place_out_body, depth),
            jax.ShapeDtypeStruct((width, 2 * out_weight.shape[1]), jnp.bfloat16),
            [meta, mine_all, to_core(mine_all), peer_all, to_core(peer_all)],
            0,
            "place_out_weight",
        )
        attended = vmem_call(
            out_body,
            jax.ShapeDtypeStruct((rows, width), jnp.bfloat16),
            [meta, spatial[0], peer, core_heads, temporal_heads, weight],
            4 * rows * width * out_weight.shape[1],
            "out_projection",
            [pltpu.VMEM((rows, 2 * out_weight.shape[1]), jnp.bfloat16)],
        )
        return attended.reshape(1, rows, width)

    def by_core(mine, other, axis):
        return jnp.where(
            core == 0,
            jnp.concatenate([mine, other], axis=axis),
            jnp.concatenate([other, mine], axis=axis),
        )

    if n_st == 2:
        spatial = jnp.where(st == 0, spatial, spatial[::-1])
    spatial = lax.all_to_all(spatial, "st", split_axis=0, concat_axis=0, tiled=True)
    spatial = by_core(spatial[:, 0, :, None], to_core(spatial[:, 1])[:, :, None], 2)
    heads = jnp.concatenate(
        [
            spatial.transpose(1, 0, 2, 3),
            temporal_heads.transpose(1, 3, 0, 2, 4).reshape(rows, n_st, 2, HEAD),
        ],
        axis=2,
    ).reshape(rows, -1)
    weight = lax.all_gather(jnp.concatenate(out_groups), "st", axis=1, tiled=True)
    weight = by_core(
        weight.reshape(chips, 1, depth, -1), to_core(weight).reshape(chips, 1, depth, -1), 1
    )
    order = jnp.zeros((chips,), jnp.int32).at[sources].set(jnp.arange(chips, dtype=jnp.int32))
    weight = weight[order].reshape(width, -1)
    attended = lax.dot_general(
        heads, weight, (((1,), (1,)), ((), ())), preferred_element_type=jnp.float32
    ).astype(jnp.bfloat16)
    return attended.reshape(1, rows, width)


def solution(mesh):
    return jax.shard_map(
        functools.partial(shards, mesh.shape["st"], mesh.shape["fsdp"]),
        mesh=mesh,
        in_specs=(P("fsdp", None, None), P("fsdp", "st", None), P("fsdp", "st"), P()),
        out_specs=P("fsdp", "st", None),
        check_vma=False,
    )
```

```python
import functools
import math

import jax
import jax.numpy as jnp
from jax import lax
from jax.experimental import pallas as pl
from jax.experimental.pallas import tpu as pltpu
from jax.sharding import PartitionSpec as P

HEAD = 128
HS_DEV = 2
SCALE = 1.0 / math.sqrt(HEAD)
MIB = 1024 * 1024
FIRST = 25_000_000_000


def kernel_call(body, out_shape, args, flops, name, whole=(), scratch=(), limit=16 * MIB):
    bytes_moved = sum(a.size * a.dtype.itemsize for a in args)

    def space(i, a):
        if a.dtype == jnp.int32:
            return pltpu.SMEM
        return pltpu.VMEM if i in whole else pl.ANY

    return pl.pallas_call(
        body,
        out_shape=out_shape,
        in_specs=[pl.BlockSpec(memory_space=space(i, a)) for i, a in enumerate(args)],
        out_specs=pl.BlockSpec(memory_space=pltpu.VMEM),
        scratch_shapes=list(scratch),
        compiler_params=pltpu.CompilerParams(vmem_limit_bytes=limit),
        cost_estimate=pl.CostEstimate(flops=flops, bytes_accessed=bytes_moved, transcendentals=0),
        name=name,
    )(*args)


def weight_copies(depth, meta_ref, piece_refs, weight, sems):
    core = meta_ref[0]
    columns = weight.shape[1]
    slot, first = 0, 0
    copies = []
    for ref in piece_refs:
        rows = min(depth, ref.shape[0])
        for start in range(0, ref.shape[0], rows):
            chip = meta_ref[2 + slot]
            for k in range(2):
                at = (chip * 2 + (core if k == 0 else 1 - core)) * depth + first
                copies.append(
                    pltpu.make_async_copy(
                        ref.at[pl.ds(start, rows), pl.ds(k * columns, columns)],
                        weight.at[pl.ds(pl.multiple_of(at, 16), rows), :],
                        sems.at[len(copies)],
                    )
                )
            first += rows
            if first == depth:
                slot, first = slot + 1, 0
    return copies


def load_all(depth, meta_ref, own_ref, other_ref, piece_refs, weight, frames, sems):
    copies = weight_copies(depth, meta_ref, piece_refs, weight, sems)
    copies.append(pltpu.make_async_copy(own_ref, frames.at[0], sems.at[len(copies)]))
    last = pltpu.make_async_copy(other_ref, frames.at[1], sems.at[len(copies)])
    for copy in copies:
        copy.start()
    last.start()
    for copy in copies:
        copy.wait()
    return last


def load_scratch(copies, patches, width):
    return [
        pltpu.VMEM((width, 3 * HEAD), jnp.bfloat16),
        pltpu.VMEM((2, patches, width), jnp.bfloat16),
        pltpu.SemaphoreType.DMA((copies + 2,)),
    ]


def most_body(depth, meta_ref, own_ref, other_ref, *refs):
    *piece_refs, out_ref, weight, frames, sems = refs
    missing = meta_ref[2 + len(piece_refs)] * 2 * depth
    weight[pl.ds(pl.multiple_of(missing, 16), 2 * depth), :] = jnp.zeros(
        (2 * depth, weight.shape[1]), weight.dtype
    )
    last = load_all(depth, meta_ref, own_ref, other_ref, piece_refs, weight, frames, sems)
    patches = own_ref.shape[0]
    half = patches // 2
    for frame in range(2):
        if frame == 1:
            last.wait()
        for first in range(0, patches, half):
            out_ref[frame * patches + first : frame * patches + first + half, :] = jnp.dot(
                frames[frame, first : first + half, :],
                weight[...],
                preferred_element_type=jnp.float32,
            )


def rest_body(depth, chips, n_st, direct, meta_ref, own_ref, other_ref, piece_ref, most_ref, *refs):
    out_ref, weight, frames, sems = refs
    patches = own_ref.shape[0]
    part = patches // (n_st * chips)
    if own_ref.shape[1] != 2 * depth:
        share = pl.ds(pl.multiple_of(meta_ref[1 + chips] * 2 * depth, 2 * depth), 2 * depth)
        own_ref, other_ref = own_ref.at[:, share], other_ref.at[:, share]
    copies = [
        pltpu.make_async_copy(ref, frames.at[k], sems.at[k])
        for k, ref in enumerate((own_ref, other_ref))
    ]
    for copy in copies:
        copy.start()
    core = meta_ref[0]
    columns = weight.shape[1]
    for k in range(2):
        at = (core if k == 0 else 1 - core) * depth
        weight[pl.ds(pl.multiple_of(at, 16), depth), :] = piece_ref[
            :, k * columns : (k + 1) * columns
        ]
    half = patches // 2
    for frame in range(2):
        copies[frame].wait()
        for first in range(0, patches, half):
            here = slice(frame * patches + first, frame * patches + first + half)
            result = most_ref[here, :] + jnp.dot(
                frames[frame, first : first + half, :],
                weight[...],
                preferred_element_type=jnp.float32,
            )
            result = result.astype(jnp.bfloat16)
            if not direct:
                out_ref[here, :] = result
                continue
            for at in range(first, first + half, part):
                block = at // part
                out_ref[block % chips, frame, block // chips] = result[
                    at - first : at - first + part
                ]


def spatial_body(depth, n_st, meta_ref, own_ref, other_ref, *refs):
    *piece_refs, out_ref, weight, frames, sems, packed = refs
    last = load_all(depth, meta_ref, own_ref, other_ref, piece_refs, weight, frames, sems)
    patches = own_ref.shape[0]
    part = patches // n_st
    half = patches // 2
    for frame in range(2):
        if frame == 1:
            last.wait()
        for first in range(0, patches, half):
            packed[first : first + half, :] = jnp.dot(
                frames[frame, first : first + half, :],
                weight[...],
                preferred_element_type=jnp.float32,
            ).astype(jnp.bfloat16)
        for group in range(n_st):
            rows = slice(group * part, (group + 1) * part)
            scores = lax.dot_general(
                packed[rows, :HEAD],
                packed[:, HEAD : 2 * HEAD],
                (((1,), (1,)), ((), ())),
                preferred_element_type=jnp.float32,
            )
            scores = scores * SCALE
            expo = jnp.exp(scores - jnp.max(scores, axis=-1, keepdims=True))
            total = jnp.sum(expo, axis=-1, keepdims=True)
            result = jnp.dot(
                expo.astype(jnp.bfloat16),
                packed[:, 2 * HEAD :],
                preferred_element_type=jnp.float32,
            )
            result = (result / total).astype(jnp.bfloat16)
            place = (group + meta_ref[1]) % 2 if n_st == 2 else group
            out_ref[place, frame] = result


def temporal_body(tile, meta_ref, qkv_ref, out_ref):
    frames, rows = qkv_ref.shape[0], qkv_ref.shape[1]
    part = out_ref.shape[2]
    flip = meta_ref[frames]
    size = frames * tile
    row_at = lax.broadcasted_iota(jnp.int32, (size, size), 0)
    col_at = lax.broadcasted_iota(jnp.int32, (size, size), 1)
    row_seg = jnp.zeros((size, 1), jnp.int32)
    col_seg = jnp.zeros((1, size), jnp.int32)
    row_frame = lax.broadcasted_iota(jnp.int32, (size, 1), 0) // tile
    col_frame = lax.broadcasted_iota(jnp.int32, (1, size), 1) // tile
    for frame in range(frames):
        clip = meta_ref[frame]
        row_seg = jnp.where(row_frame == frame, clip, row_seg)
        col_seg = jnp.where(col_frame == frame, clip, col_seg)
    keep = (row_at % tile == col_at % tile) & (row_seg == col_seg)
    for start in range(0, rows, tile):
        block = qkv_ref[:, start : start + tile, :].reshape(size, 3 * HEAD)
        scores = lax.dot_general(
            block[:, :HEAD],
            block[:, HEAD : 2 * HEAD],
            (((1,), (1,)), ((), ())),
            preferred_element_type=jnp.float32,
        )
        scores = jnp.where(keep, scores * SCALE, jnp.float32(-1e30))
        expo = jnp.exp(scores - jnp.max(scores, axis=-1, keepdims=True))
        total = jnp.sum(expo, axis=-1, keepdims=True)
        result = jnp.dot(
            expo.astype(jnp.bfloat16), block[:, 2 * HEAD :], preferred_element_type=jnp.float32
        )
        result = (result / total).astype(jnp.bfloat16).reshape(frames, tile, HEAD)
        for pair in range(frames // 2):
            for k in range(2):
                at = 2 * pair + (flip if k == 0 else 1 - flip)
                if part % tile:
                    out_ref[0, at, start : start + tile, :] = result[2 * pair + k]
                else:
                    low = start % part
                    out_ref[start // part, at, low : low + tile, :] = result[2 * pair + k]


def pack_body(split, *refs):
    *piece_refs, out_ref, sems = refs
    copies = []
    for i, ref in enumerate(piece_refs):
        rows, columns = ref.shape
        copies.append(
            pltpu.make_async_copy(
                ref.at[:, pl.ds(split, columns - split)],
                out_ref.at[pl.ds(i * rows, rows), :],
                sems.at[i],
            )
        )
    for copy in copies:
        copy.start()
    for copy in copies:
        copy.wait()


def order_body(received_ref, out_ref):
    n_st, chips, _, part, _ = received_ref.shape
    for group in range(n_st):
        for chip in range(chips):
            for k in range(2):
                out_ref[
                    group, chip * part : (chip + 1) * part, k * HEAD : (k + 1) * HEAD
                ] = received_ref[group, chip, k]


def out_body(
    depth, count, meta_ref, mine_ref, peer_ref, core_ref, far_ref, temporal_ref, *refs
):
    *weight_refs, out_ref, heads, weight, sems = refs
    core, st = meta_ref[0], meta_ref[1]
    n_st, chips = temporal_ref.shape[0], out_ref.shape[1] // (2 * depth)
    copies = [[] for _ in range(chips)]
    for kind in range(4):
        group = st if kind < 2 else 1 - st
        side = core if kind % 2 == 0 else 1 - core
        slot = 0
        for ref in weight_refs[kind * count : (kind + 1) * count]:
            for first in range(0, ref.shape[0], depth):
                at = slot * 2 * depth + side * depth
                copies[slot].append(
                    pltpu.make_async_copy(
                        ref.at[pl.ds(first, depth), :],
                        weight.at[group, pl.ds(pl.multiple_of(at, 16), depth), :],
                        sems.at[slot, kind],
                    )
                )
                slot += 1
    for copy in sum(copies, []):
        copy.start()
    mine, far = pl.multiple_of(core * HEAD, HEAD), pl.multiple_of((1 - core) * HEAD, HEAD)
    heads[st, :, pl.ds(mine, HEAD)] = mine_ref[...]
    heads[1 - st, :, pl.ds(mine, HEAD)] = peer_ref[...]
    heads[st, :, pl.ds(far, HEAD)] = core_ref[...]
    heads[1 - st, :, pl.ds(far, HEAD)] = far_ref[...]
    heads[:, :, HS_DEV * HEAD :] = temporal_ref[...]
    chip_width = 2 * depth
    for slot in range(0, chips, 2):
        for copy in copies[slot] + copies[slot + 1]:
            copy.wait()
        total = 0.0
        for group in range(n_st):
            total += lax.dot_general(
                heads[group],
                weight[group, slot * chip_width : (slot + 2) * chip_width, :],
                (((1,), (1,)), ((), ())),
                preferred_element_type=jnp.float32,
            )
        total = total.astype(jnp.bfloat16)
        for k in range(2):
            at = pl.multiple_of(meta_ref[2 + slot + k] * chip_width, chip_width)
            out_ref[:, pl.ds(at, chip_width)] = total[:, k * chip_width : (k + 1) * chip_width]


def shards(n_st, n_fsdp, normed, qkv_weight, out_weight, segment_ids):
    patches, width = normed.shape[1], normed.shape[2]
    frames = n_fsdp
    depth = qkv_weight.shape[0]
    chips = n_fsdp // 2
    part = patches // (n_st * chips)
    rows = patches // n_st
    direct = part % 16 == 0
    ring = list(range(0, chips, 2)) + list(range(chips - 1, 0, -2))
    place = [ring.index(chip) for chip in range(chips)]
    me = lax.axis_index("fsdp")
    st = lax.axis_index("st")
    chip, core = me // 2, me % 2
    spot = jnp.array(place, jnp.int32)[chip]

    swap = [(i, i ^ 1) for i in range(n_fsdp)]
    forward = [
        (2 * ring[i] + c, 2 * ring[(i + 1) % chips] + c) for i in range(chips) for c in range(2)
    ]
    backward = [(b, a) for a, b in forward]

    def to_core(x):
        return lax.ppermute(x, "fsdp", swap)

    def to_peer(x):
        return lax.ppermute(x, "st", [(0, 1), (1, 0)])

    def ring_gather(piece):
        pieces = [piece]
        ahead = behind = piece
        for _ in range(1, chips // 2):
            gate = yield pieces, ahead
            if gate is not None:
                ahead, behind, _ = lax.optimization_barrier((ahead, behind, gate))
            ahead = lax.ppermute(ahead, "fsdp", forward)
            behind = lax.ppermute(behind, "fsdp", backward)
            pieces = pieces + [ahead, behind]
        sent = jnp.where(core == 0, ahead, behind)
        gate = yield pieces, sent
        if gate is not None:
            sent, _ = lax.optimization_barrier((sent, gate))
        both = [edge for edge in forward if edge[0] % 2 == 0]
        both += [edge for edge in backward if edge[0] % 2 == 1]
        yield pieces + [lax.ppermute(sent, "fsdp", both)], None

    def run(ring, steps):
        for _ in range(steps):
            state = next(ring)
        return state

    offsets = [0]
    for d in range(1, chips // 2):
        offsets += [chips - d, d]
    offsets.append(chips // 2)
    sources = jnp.array(ring, jnp.int32)[(spot + jnp.array(offsets, jnp.int32)) % chips]
    here = jnp.stack([core, st])
    ring_meta = jnp.concatenate([here, sources]).astype(jnp.int32)

    by_head = qkv_weight.transpose(1, 0, 2)

    def take_head(heads):
        mine = lax.dynamic_index_in_dim(heads, core, 0, keepdims=False)
        other = lax.dynamic_index_in_dim(heads, 1 - core, 0, keepdims=False)
        return jnp.concatenate([mine, to_core(other)], axis=1)

    temporal_piece = take_head(lax.optimization_barrier(by_head[HS_DEV:]))
    own = normed.reshape(patches, width)

    temporal_ring = ring_gather(temporal_piece)
    _, last_sent = run(temporal_ring, chips // 2)
    pieces, _ = next(temporal_ring)
    own, later_head, _ = lax.optimization_barrier((own, by_head[:HS_DEV], temporal_piece))
    other = to_core(own)
    spatial_piece = take_head(later_head)
    split = spatial_piece.shape[1]
    both_ring = ring_gather(jnp.concatenate([spatial_piece, out_weight], axis=1))
    next(both_ring)
    first_pieces, _ = both_ring.send(last_sent)
    head_flops = 4 * patches * width * 3 * HEAD
    shape = (chips, 2, n_st, part, 3 * HEAD) if direct else (2 * patches, 3 * HEAD)
    most = kernel_call(
        functools.partial(most_body, depth),
        jax.ShapeDtypeStruct((2 * patches, 3 * HEAD), jnp.float32),
        [ring_meta, own, other, *pieces[:-1]],
        head_flops,
        "temporal_projection",
        scratch=load_scratch(2 * chips, patches, width),
    )
    shares = (own, other)
    if 2 * depth % 128:
        shares = [
            lax.dynamic_slice_in_dim(x, sources[-1] * 2 * depth, 2 * depth, 1) for x in shares
        ]
    temporal = projected = kernel_call(
        functools.partial(rest_body, depth, chips, n_st, direct),
        jax.ShapeDtypeStruct(shape, jnp.bfloat16),
        [ring_meta, *shares, pieces[-1], most],
        head_flops // chips,
        "temporal_projection_rest",
        whole=(3, 4),
        scratch=[
            pltpu.VMEM((2 * depth, 3 * HEAD), jnp.bfloat16),
            pltpu.VMEM((2, patches, 2 * depth), jnp.bfloat16),
            pltpu.SemaphoreType.DMA((2,)),
        ],
    )
    if not direct:
        temporal = temporal.reshape(2, n_st, chips, part, 3 * HEAD).transpose(2, 0, 1, 3, 4)
    same_core = [[2 * i + c for i in range(chips)] for c in range(2)]
    temporal = lax.all_to_all(
        temporal,
        "fsdp",
        split_axis=0,
        concat_axis=0,
        tiled=True,
        axis_index_groups=same_core,
    ).reshape(frames, n_st * part, 3 * HEAD)
    pairs = segment_ids.reshape(chips, 2)
    pairs = jnp.where(core == 0, pairs, pairs[:, ::-1]).reshape(frames)
    clips = jnp.concatenate([pairs, core.reshape(1)]).astype(jnp.int32)
    tile = min(n_st * part, max(16, 256 // frames))
    if part % tile == 0:
        shape = (n_st, frames, part, HEAD)
    else:
        shape = (1, frames, n_st * part, HEAD)
    result = attention = kernel_call(
        functools.partial(temporal_body, tile),
        jax.ShapeDtypeStruct(shape, jnp.bfloat16),
        [clips, temporal],
        FIRST,
        "temporal_attention",
        whole=(1,),
    )
    if part % tile:
        result = result.reshape(frames, n_st, part, HEAD).transpose(1, 0, 2, 3)
    result = lax.all_to_all(
        result.reshape(n_st * frames, part, HEAD),
        ("st", "fsdp"),
        split_axis=0,
        concat_axis=0,
        tiled=True,
    )
    temporal_heads = result.reshape(n_st, chips, 2, part, HEAD)

    def pack(group):
        return kernel_call(
            functools.partial(pack_body, split),
            jax.ShapeDtypeStruct((depth * len(group), out_weight.shape[1]), jnp.bfloat16),
            group,
            0,
            "pack_out_weight",
            scratch=[pltpu.SemaphoreType.DMA((len(group),))],
            limit=60 * MIB,
        )

    early = n_st == 2 and direct
    parts, _ = both_ring.send(projected)
    if early:
        kinds = [pack(parts[:3]), pack(parts[3:5])]
        peers = [to_peer(k) for k in kinds]
    parts, _ = run(both_ring, chips // 2 - 3)
    parts, _ = both_ring.send(tuple(peers) if early else attention)
    spatial = kernel_call(
        functools.partial(spatial_body, depth, n_st),
        jax.ShapeDtypeStruct((n_st, 2, rows, HEAD), jnp.bfloat16),
        [ring_meta, own, other, *parts],
        0,
        "spatial_heads",
        scratch=[
            *load_scratch(2 * chips + 2, patches, width),
            pltpu.VMEM((patches, 3 * HEAD), jnp.bfloat16),
        ],
    )

    if early:
        temporal_heads = kernel_call(
            order_body,
            jax.ShapeDtypeStruct((n_st, rows, 2 * HEAD), jnp.bfloat16),
            [temporal_heads],
            FIRST,
            "temporal_heads",
            whole=(0,),
        )
        across = [(i, (i ^ 1 ^ n_fsdp)) for i in range(n_st * n_fsdp)]
        received = [
            to_peer(spatial[1, 0]),
            to_core(spatial[0, 1]),
            lax.ppermute(spatial[1, 1], ("st", "fsdp"), across),
        ]

        kinds += [pack(parts[at : at + 2]) for at in range(5, chips, 2)]
        peers += [to_peer(k) for k in kinds[2:]]
        count = len(kinds)
        kinds += [to_core(k) for k in kinds] + peers
        peers = lax.optimization_barrier((*peers, attention))[:-1]
        kinds += [to_core(k) for k in peers]
        attended = kernel_call(
            functools.partial(out_body, depth, count),
            jax.ShapeDtypeStruct((rows, width), jnp.bfloat16),
            [ring_meta, spatial[0, 0], *received, temporal_heads, *kinds],
            4 * rows * width * out_weight.shape[1],
            "out_projection",
            whole=(1, 2, 3, 4, 5),
            scratch=[
                pltpu.VMEM((n_st, rows, out_weight.shape[1]), jnp.bfloat16),
                pltpu.VMEM((n_st, width, out_weight.shape[1]), jnp.bfloat16),
                pltpu.SemaphoreType.DMA((chips, 4)),
            ],
            limit=60 * MIB,
        )
        return attended.reshape(1, rows, width)

    def by_core(mine, other, axis):
        return jnp.where(
            core == 0,
            jnp.concatenate([mine, other], axis=axis),
            jnp.concatenate([other, mine], axis=axis),
        )

    if n_st == 2:
        spatial = jnp.where(st == 0, spatial, spatial[::-1])
    spatial = lax.all_to_all(spatial, "st", split_axis=0, concat_axis=0, tiled=True)
    spatial = by_core(spatial[:, 0, :, None], to_core(spatial[:, 1])[:, :, None], 2)
    heads = jnp.concatenate(
        [
            spatial.transpose(1, 0, 2, 3),
            temporal_heads.transpose(1, 3, 0, 2, 4).reshape(rows, n_st, 2, HEAD),
        ],
        axis=2,
    ).reshape(rows, -1)
    weight = jnp.concatenate([p[:, split:] for p in parts])
    weight = lax.all_gather(weight, "st", axis=1, tiled=True)
    weight = by_core(
        weight.reshape(chips, 1, depth, -1), to_core(weight).reshape(chips, 1, depth, -1), 1
    )
    order = jnp.zeros((chips,), jnp.int32).at[sources].set(jnp.arange(chips, dtype=jnp.int32))
    attended = lax.dot_general(
        heads,
        weight[order].reshape(width, -1),
        (((1,), (1,)), ((), ())),
        preferred_element_type=jnp.float32,
    ).astype(jnp.bfloat16)
    return attended.reshape(1, rows, width)


def solution(mesh):
    return jax.shard_map(
        functools.partial(shards, mesh.shape["st"], mesh.shape["fsdp"]),
        mesh=mesh,
        in_specs=(P("fsdp", None, None), P("fsdp", "st", None), P("fsdp", "st"), P()),
        out_specs=P("fsdp", "st", None),
        check_vma=False,
    )
```

```python
import functools
import math

import jax
import jax.numpy as jnp
from jax import lax
from jax.experimental import pallas as pl
from jax.experimental.pallas import tpu as pltpu
from jax.sharding import PartitionSpec as P

HEAD = 128
HS_DEV = 2
SCALE = 1.0 / math.sqrt(HEAD)
CFG = dict(A=1, B=3, C=1, D1=5, D2=5, F=2, G=1, H=3, I=0, MT=1, MS=3, K=0)
MIB = 1024 * 1024
FIRST = 25_000_000_000


def kernel_call(body, out_shape, args, flops, name, whole=(), scratch=(), limit=16 * MIB):
    bytes_moved = sum(a.size * a.dtype.itemsize for a in args)

    def space(i, a):
        if a.dtype == jnp.int32:
            return pltpu.SMEM
        return pltpu.VMEM if i in whole else pl.ANY

    return pl.pallas_call(
        body,
        out_shape=out_shape,
        in_specs=[pl.BlockSpec(memory_space=space(i, a)) for i, a in enumerate(args)],
        out_specs=pl.BlockSpec(memory_space=pltpu.VMEM),
        scratch_shapes=list(scratch),
        compiler_params=pltpu.CompilerParams(vmem_limit_bytes=limit),
        cost_estimate=pl.CostEstimate(flops=flops, bytes_accessed=bytes_moved, transcendentals=0),
        name=name,
    )(*args)


def weight_copies(depth, meta_ref, piece_refs, weight, sems):
    core = meta_ref[0]
    columns = weight.shape[1]
    slot, first = 0, 0
    copies = []
    for ref in piece_refs:
        rows = min(depth, ref.shape[0])
        for start in range(0, ref.shape[0], rows):
            chip = meta_ref[2 + slot]
            for k in range(2):
                at = (chip * 2 + (core if k == 0 else 1 - core)) * depth + first
                copies.append(
                    pltpu.make_async_copy(
                        ref.at[pl.ds(start, rows), pl.ds(k * columns, columns)],
                        weight.at[pl.ds(pl.multiple_of(at, 16), rows), :],
                        sems.at[len(copies)],
                    )
                )
            first += rows
            if first == depth:
                slot, first = slot + 1, 0
    return copies


def load_all(depth, meta_ref, own_ref, other_ref, piece_refs, weight, frames, sems):
    copies = weight_copies(depth, meta_ref, piece_refs, weight, sems)
    copies.append(pltpu.make_async_copy(own_ref, frames.at[0], sems.at[len(copies)]))
    last = pltpu.make_async_copy(other_ref, frames.at[1], sems.at[len(copies)])
    for copy in copies:
        copy.start()
    last.start()
    for copy in copies:
        copy.wait()
    return last


def load_scratch(copies, patches, width):
    return [
        pltpu.VMEM((width, 3 * HEAD), jnp.bfloat16),
        pltpu.VMEM((2, patches, width), jnp.bfloat16),
        pltpu.SemaphoreType.DMA((copies + 2,)),
    ]


def most_body(depth, meta_ref, own_ref, other_ref, *refs):
    *piece_refs, out_ref, weight, frames, sems = refs
    for slot in range(len(piece_refs), weight.shape[0] // (2 * depth)):
        missing = meta_ref[2 + slot] * 2 * depth
        weight[pl.ds(pl.multiple_of(missing, 16), 2 * depth), :] = jnp.zeros(
            (2 * depth, weight.shape[1]), weight.dtype
        )
    last = load_all(depth, meta_ref, own_ref, other_ref, piece_refs, weight, frames, sems)
    patches = own_ref.shape[0]
    half = patches // 2
    for frame in range(2):
        if frame == 1:
            last.wait()
        for first in range(0, patches, half):
            out_ref[frame * patches + first : frame * patches + first + half, :] = jnp.dot(
                frames[frame, first : first + half, :],
                weight[...],
                preferred_element_type=jnp.float32,
            )


def add_rest(depth, chips, meta_ref, own_ref, other_ref, most_ref, piece_refs, weight, frames, sems):
    patches = own_ref.shape[0]
    late = len(piece_refs)
    copies = [[], []]
    for k, ref in enumerate((own_ref, other_ref)):
        if ref.shape[1] == frames.shape[2]:
            copies[k].append(pltpu.make_async_copy(ref, frames.at[k], sems.at[k, 0]))
            continue
        for i in range(late):
            at = meta_ref[2 + chips - late + i] * 2 * depth
            copies[k].append(
                pltpu.make_async_copy(
                    ref.at[:, pl.ds(pl.multiple_of(at, 2 * depth), 2 * depth)],
                    frames.at[k, :, pl.ds(i * 2 * depth, 2 * depth)],
                    sems.at[k, i],
                )
            )
    for copy in copies[0] + copies[1]:
        copy.start()
    core = meta_ref[0]
    columns = weight.shape[1]
    for i, piece_ref in enumerate(piece_refs):
        for k in range(2):
            at = (2 * i + (core if k == 0 else 1 - core)) * depth
            weight[pl.ds(pl.multiple_of(at, 16), depth), :] = piece_ref[
                :, k * columns : (k + 1) * columns
            ]
    half = patches // 2
    for frame in range(2):
        for copy in copies[frame]:
            copy.wait()
        for first in range(0, patches, half):
            here = slice(frame * patches + first, frame * patches + first + half)
            result = most_ref[here, :] + jnp.dot(
                frames[frame, first : first + half, :],
                weight[...],
                preferred_element_type=jnp.float32,
            )
            yield frame, first, result.astype(jnp.bfloat16)


def rest_body(depth, chips, n_st, direct, late, meta_ref, own_ref, other_ref, most_ref, *refs):
    piece_refs, (out_ref, *scratch) = refs[:late], refs[late:]
    patches = own_ref.shape[0]
    part = patches // (n_st * chips)
    for frame, first, result in add_rest(
        depth, chips, meta_ref, own_ref, other_ref, most_ref, piece_refs, *scratch
    ):
        rows = result.shape[0]
        if not direct:
            out_ref[frame * patches + first : frame * patches + first + rows, :] = result
            continue
        for at in range(first, first + rows, part):
            block = at // part
            out_ref[block % chips, frame, block // chips] = result[at - first : at - first + part]


def spatial_body(depth, chips, n_st, late, meta_ref, own_ref, other_ref, most_ref, *refs):
    piece_refs, (out_ref, *scratch, packed) = refs[:late], refs[late:]
    patches = own_ref.shape[0]
    part = patches // n_st
    for frame, first, result in add_rest(
        depth, chips, meta_ref, own_ref, other_ref, most_ref, piece_refs, *scratch
    ):
        packed[first : first + result.shape[0], :] = result
        if first + result.shape[0] < patches:
            continue
        for group in range(n_st):
            rows = slice(group * part, (group + 1) * part)
            scores = lax.dot_general(
                packed[rows, :HEAD],
                packed[:, HEAD : 2 * HEAD],
                (((1,), (1,)), ((), ())),
                preferred_element_type=jnp.float32,
            )
            scores = scores * SCALE
            expo = jnp.exp(scores - jnp.max(scores, axis=-1, keepdims=True))
            total = jnp.sum(expo, axis=-1, keepdims=True)
            result = jnp.dot(
                expo.astype(jnp.bfloat16),
                packed[:, 2 * HEAD :],
                preferred_element_type=jnp.float32,
            )
            result = (result / total).astype(jnp.bfloat16)
            place = (group + meta_ref[1]) % 2 if n_st == 2 else group
            out_ref[place, frame] = result


def temporal_body(tile, meta_ref, qkv_ref, out_ref):
    frames, rows = qkv_ref.shape[0], qkv_ref.shape[1]
    part = out_ref.shape[2]
    flip = meta_ref[frames]
    size = frames * tile
    row_at = lax.broadcasted_iota(jnp.int32, (size, size), 0)
    col_at = lax.broadcasted_iota(jnp.int32, (size, size), 1)
    row_seg = jnp.zeros((size, 1), jnp.int32)
    col_seg = jnp.zeros((1, size), jnp.int32)
    row_frame = lax.broadcasted_iota(jnp.int32, (size, 1), 0) // tile
    col_frame = lax.broadcasted_iota(jnp.int32, (1, size), 1) // tile
    for frame in range(frames):
        clip = meta_ref[frame]
        row_seg = jnp.where(row_frame == frame, clip, row_seg)
        col_seg = jnp.where(col_frame == frame, clip, col_seg)
    keep = (row_at % tile == col_at % tile) & (row_seg == col_seg)
    for start in range(0, rows, tile):
        block = qkv_ref[:, start : start + tile, :].reshape(size, 3 * HEAD)
        scores = lax.dot_general(
            block[:, :HEAD],
            block[:, HEAD : 2 * HEAD],
            (((1,), (1,)), ((), ())),
            preferred_element_type=jnp.float32,
        )
        scores = jnp.where(keep, scores * SCALE, jnp.float32(-1e30))
        expo = jnp.exp(scores - jnp.max(scores, axis=-1, keepdims=True))
        total = jnp.sum(expo, axis=-1, keepdims=True)
        result = jnp.dot(
            expo.astype(jnp.bfloat16), block[:, 2 * HEAD :], preferred_element_type=jnp.float32
        )
        result = (result / total).astype(jnp.bfloat16).reshape(frames, tile, HEAD)
        for pair in range(frames // 2):
            for k in range(2):
                at = 2 * pair + (flip if k == 0 else 1 - flip)
                if part % tile:
                    out_ref[0, at, start : start + tile, :] = result[2 * pair + k]
                else:
                    low = start % part
                    out_ref[start // part, at, low : low + tile, :] = result[2 * pair + k]


def pack_body(split, *refs):
    *piece_refs, out_ref, sems = refs
    copies = []
    for i, ref in enumerate(piece_refs):
        rows, columns = ref.shape
        copies.append(
            pltpu.make_async_copy(
                ref.at[:, pl.ds(split, columns - split)],
                out_ref.at[pl.ds(i * rows, rows), :],
                sems.at[i],
            )
        )
    for copy in copies:
        copy.start()
    for copy in copies:
        copy.wait()


def order_body(received_ref, out_ref):
    n_st, chips, _, part, _ = received_ref.shape
    for group in range(n_st):
        for chip in range(chips):
            for k in range(2):
                out_ref[
                    group, chip * part : (chip + 1) * part, k * HEAD : (k + 1) * HEAD
                ] = received_ref[group, chip, k]


def out_body(
    depth, count, meta_ref, mine_ref, peer_ref, core_ref, far_ref, temporal_ref, *refs
):
    *weight_refs, out_ref, heads, weight, sems = refs
    core, st = meta_ref[0], meta_ref[1]
    n_st, chips = temporal_ref.shape[0], out_ref.shape[1] // (2 * depth)
    copies = [[] for _ in range(chips)]
    for kind in range(4):
        group = st if kind < 2 else 1 - st
        side = core if kind % 2 == 0 else 1 - core
        slot = 0
        for ref in weight_refs[kind * count : (kind + 1) * count]:
            for first in range(0, ref.shape[0], depth):
                at = slot * 2 * depth + side * depth
                copies[slot].append(
                    pltpu.make_async_copy(
                        ref.at[pl.ds(first, depth), :],
                        weight.at[group, pl.ds(pl.multiple_of(at, 16), depth), :],
                        sems.at[slot, kind],
                    )
                )
                slot += 1
    for copy in sum(copies, []):
        copy.start()
    mine, far = pl.multiple_of(core * HEAD, HEAD), pl.multiple_of((1 - core) * HEAD, HEAD)
    heads[st, :, pl.ds(mine, HEAD)] = mine_ref[...]
    heads[1 - st, :, pl.ds(mine, HEAD)] = peer_ref[...]
    heads[st, :, pl.ds(far, HEAD)] = core_ref[...]
    heads[1 - st, :, pl.ds(far, HEAD)] = far_ref[...]
    heads[:, :, HS_DEV * HEAD :] = temporal_ref[...]
    chip_width = 2 * depth
    for slot in range(0, chips, 2):
        for copy in copies[slot] + copies[slot + 1]:
            copy.wait()
        total = 0.0
        for group in range(n_st):
            total += lax.dot_general(
                heads[group],
                weight[group, slot * chip_width : (slot + 2) * chip_width, :],
                (((1,), (1,)), ((), ())),
                preferred_element_type=jnp.float32,
            )
        total = total.astype(jnp.bfloat16)
        for k in range(2):
            at = pl.multiple_of(meta_ref[2 + slot + k] * chip_width, chip_width)
            out_ref[:, pl.ds(at, chip_width)] = total[:, k * chip_width : (k + 1) * chip_width]


def shards(n_st, n_fsdp, normed, qkv_weight, out_weight, segment_ids):
    patches, width = normed.shape[1], normed.shape[2]
    frames = n_fsdp
    depth = qkv_weight.shape[0]
    chips = n_fsdp // 2
    part = patches // (n_st * chips)
    rows = patches // n_st
    direct = part % 16 == 0
    ring = list(range(0, chips, 2)) + list(range(chips - 1, 0, -2))
    place = [ring.index(chip) for chip in range(chips)]
    me = lax.axis_index("fsdp")
    st = lax.axis_index("st")
    chip, core = me // 2, me % 2
    spot = jnp.array(place, jnp.int32)[chip]

    swap = [(i, i ^ 1) for i in range(n_fsdp)]
    forward = [
        (2 * ring[i] + c, 2 * ring[(i + 1) % chips] + c) for i in range(chips) for c in range(2)
    ]
    backward = [(b, a) for a, b in forward]

    def to_core(x):
        return lax.ppermute(x, "fsdp", swap)

    def to_peer(x):
        return lax.ppermute(x, "st", [(0, 1), (1, 0)])

    def ring_gather(piece):
        pieces = [piece]
        ahead = behind = piece
        for _ in range(1, chips // 2):
            gate = yield pieces, ahead
            if gate is not None:
                ahead, behind, _ = lax.optimization_barrier((ahead, behind, gate))
            ahead = lax.ppermute(ahead, "fsdp", forward)
            behind = lax.ppermute(behind, "fsdp", backward)
            pieces = pieces + [ahead, behind]
        gate = yield pieces, ahead
        if gate is not None:
            ahead, behind, _ = lax.optimization_barrier((ahead, behind, gate))
        sent = jnp.where(core == 0, ahead, behind)
        gate = yield pieces, sent
        if gate is not None:
            sent, _ = lax.optimization_barrier((sent, gate))
        both = [edge for edge in forward if edge[0] % 2 == 0]
        both += [edge for edge in backward if edge[0] % 2 == 1]
        yield pieces + [lax.ppermute(sent, "fsdp", both)], None

    def run(ring, steps):
        for _ in range(steps):
            state = next(ring)
        return state

    offsets = [0]
    for d in range(1, chips // 2):
        offsets += [chips - d, d]
    offsets.append(chips // 2)
    sources = jnp.array(ring, jnp.int32)[(spot + jnp.array(offsets, jnp.int32)) % chips]
    here = jnp.stack([core, st])
    ring_meta = jnp.concatenate([here, sources]).astype(jnp.int32)

    by_head = qkv_weight.transpose(1, 0, 2)

    def take_head(heads):
        mine = lax.dynamic_index_in_dim(heads, core, 0, keepdims=False)
        other = lax.dynamic_index_in_dim(heads, 1 - core, 0, keepdims=False)
        return jnp.concatenate([mine, to_core(other)], axis=1)

    temporal_piece = take_head(lax.optimization_barrier(by_head[HS_DEV:]))
    own = normed.reshape(patches, width)

    temporal_ring = ring_gather(temporal_piece)
    second_pieces, _ = run(temporal_ring, 3)
    third_pieces, _ = run(temporal_ring, chips // 2 - 3)
    _, last_sent = run(temporal_ring, 1)
    pieces, _ = next(temporal_ring)
    own, later_head, _ = lax.optimization_barrier((own, by_head[:HS_DEV], temporal_piece))
    other = to_core(own)
    spatial_piece = take_head(later_head)
    split = spatial_piece.shape[1]
    both_ring = ring_gather(jnp.concatenate([spatial_piece, out_weight], axis=1))
    next(both_ring)
    first_pieces, _ = both_ring.send([None, last_sent, third_pieces[-1], second_pieces[-1]][CFG['H']])
    temporal_late, spatial_late = CFG['MT'], CFG['MS']
    head_flops = 4 * patches * width * 3 * HEAD
    shape = (chips, 2, n_st, part, 3 * HEAD) if direct else (2 * patches, 3 * HEAD)
    most = kernel_call(
        functools.partial(most_body, depth),
        jax.ShapeDtypeStruct((2 * patches, 3 * HEAD), jnp.float32),
        [ring_meta, own, other, *pieces[: chips - temporal_late]],
        head_flops,
        "temporal_projection",
        scratch=load_scratch(2 * chips, patches, width),
    )
    temporal_most = most
    if CFG['A']:
        most, *_ = lax.optimization_barrier((most, *first_pieces))
    def shares(late):
        if 2 * depth % 128 == 0:
            return own, other
        return [
            jnp.concatenate(
                [
                    lax.dynamic_slice_in_dim(x, sources[chips - i] * 2 * depth, 2 * depth, 1)
                    for i in range(late, 0, -1)
                ],
                axis=1,
            )
            for x in (own, other)
        ]

    def rest_scratch(late):
        return [
            pltpu.VMEM((late * 2 * depth, 3 * HEAD), jnp.bfloat16),
            pltpu.VMEM((2, patches, late * 2 * depth), jnp.bfloat16),
            pltpu.SemaphoreType.DMA((2, late)),
        ]

    temporal = projected = kernel_call(
        functools.partial(rest_body, depth, chips, n_st, direct, temporal_late),
        jax.ShapeDtypeStruct(shape, jnp.bfloat16),
        [ring_meta, *shares(temporal_late), most, *pieces[chips - temporal_late :]],
        head_flops // chips,
        "temporal_projection_rest",
        whole=range(3, 4 + temporal_late),
        scratch=rest_scratch(temporal_late),
    )
    if not direct:
        temporal = temporal.reshape(2, n_st, chips, part, 3 * HEAD).transpose(2, 0, 1, 3, 4)
    second_parts, _ = both_ring.send([None, projected, temporal_most][CFG['F']])
    if chips > 8:
        second_parts, _ = run(both_ring, chips // 2 - 4)
    spatial_most = kernel_call(
        functools.partial(most_body, depth),
        jax.ShapeDtypeStruct((2 * patches, 3 * HEAD), jnp.float32),
        [ring_meta, own, other, *second_parts[: chips - spatial_late]],
        0,
        "spatial_projection",
        scratch=load_scratch(2 * chips, patches, width),
    )
    same_core = [[2 * i + c for i in range(chips)] for c in range(2)]
    temporal = lax.all_to_all(
        temporal,
        "fsdp",
        split_axis=0,
        concat_axis=0,
        tiled=True,
        axis_index_groups=same_core,
    ).reshape(frames, n_st * part, 3 * HEAD)
    pairs = segment_ids.reshape(chips, 2)
    pairs = jnp.where(core == 0, pairs, pairs[:, ::-1]).reshape(frames)
    clips = jnp.concatenate([pairs, core.reshape(1)]).astype(jnp.int32)
    if CFG['K']:
        temporal, _ = lax.optimization_barrier((temporal, spatial_most))
    tile = min(n_st * part, max(16, 256 // frames))
    if part % tile == 0:
        shape = (n_st, frames, part, HEAD)
    else:
        shape = (1, frames, n_st * part, HEAD)
    result = attention = kernel_call(
        functools.partial(temporal_body, tile),
        jax.ShapeDtypeStruct(shape, jnp.bfloat16),
        [clips, temporal],
        CFG['D1'] * 1000000000,
        "temporal_attention",
        whole=(1,),
    )
    if part % tile:
        result = result.reshape(frames, n_st, part, HEAD).transpose(1, 0, 2, 3)
    result = lax.all_to_all(
        result.reshape(n_st * frames, part, HEAD),
        ("st", "fsdp"),
        split_axis=0,
        concat_axis=0,
        tiled=True,
    )
    temporal_heads = result.reshape(n_st, chips, 2, part, HEAD)

    def pack(group):
        return kernel_call(
            functools.partial(pack_body, split),
            jax.ShapeDtypeStruct((depth * len(group), out_weight.shape[1]), jnp.bfloat16),
            group,
            0,
            "pack_out_weight",
            scratch=[pltpu.SemaphoreType.DMA((len(group),))],
            limit=60 * MIB,
        )

    early = n_st == 2 and direct
    parts = second_parts
    if early:
        kinds = [pack(parts[:3]), pack(parts[3:5])]
        peers = [to_peer(k) for k in kinds]
    both_ring.send(attention if CFG['I'] else None)
    both_ring.send([None, attention, None, spatial_most][CFG['B']])
    late = []
    if CFG['B'] == 2:
        late.append(attention)
    if CFG['C'] == 1 and early:
        late += peers
    parts, _ = both_ring.send(tuple(late) if late else None)
    spatial = kernel_call(
        functools.partial(spatial_body, depth, chips, n_st, spatial_late),
        jax.ShapeDtypeStruct((n_st, 2, rows, HEAD), jnp.bfloat16),
        [ring_meta, *shares(spatial_late), spatial_most, *parts[chips - spatial_late :]],
        0,
        "spatial_heads",
        whole=range(3, 4 + spatial_late),
        scratch=[*rest_scratch(spatial_late), pltpu.VMEM((patches, 3 * HEAD), jnp.bfloat16)],
    )

    if early:
        temporal_heads = kernel_call(
            order_body,
            jax.ShapeDtypeStruct((n_st, rows, 2 * HEAD), jnp.bfloat16),
            [temporal_heads],
            CFG['D2'] * 1000000000,
            "temporal_heads",
            whole=(0,),
        )
        across = [(i, (i ^ 1 ^ n_fsdp)) for i in range(n_st * n_fsdp)]
        received = [
            to_peer(spatial[1, 0]),
            to_core(spatial[0, 1]),
            lax.ppermute(spatial[1, 1], ("st", "fsdp"), across),
        ]

        kinds += [pack(parts[at : at + 2]) for at in range(5, chips, 2)]
        peers += [to_peer(k) for k in kinds[2:]]
        count = len(kinds)
        kinds += [to_core(k) for k in kinds] + peers
        if CFG['G']:
            peers = lax.optimization_barrier((*peers, attention if CFG['G'] == 1 else spatial))[:-1]
        kinds += [to_core(k) for k in peers]
        attended = kernel_call(
            functools.partial(out_body, depth, count),
            jax.ShapeDtypeStruct((rows, width), jnp.bfloat16),
            [ring_meta, spatial[0, 0], *received, temporal_heads, *kinds],
            4 * rows * width * out_weight.shape[1],
            "out_projection",
            whole=(1, 2, 3, 4, 5),
            scratch=[
                pltpu.VMEM((n_st, rows, out_weight.shape[1]), jnp.bfloat16),
                pltpu.VMEM((n_st, width, out_weight.shape[1]), jnp.bfloat16),
                pltpu.SemaphoreType.DMA((chips, 4)),
            ],
            limit=60 * MIB,
        )
        return attended.reshape(1, rows, width)

    def by_core(mine, other, axis):
        return jnp.where(
            core == 0,
            jnp.concatenate([mine, other], axis=axis),
            jnp.concatenate([other, mine], axis=axis),
        )

    if n_st == 2:
        spatial = jnp.where(st == 0, spatial, spatial[::-1])
    spatial = lax.all_to_all(spatial, "st", split_axis=0, concat_axis=0, tiled=True)
    spatial = by_core(spatial[:, 0, :, None], to_core(spatial[:, 1])[:, :, None], 2)
    heads = jnp.concatenate(
        [
            spatial.transpose(1, 0, 2, 3),
            temporal_heads.transpose(1, 3, 0, 2, 4).reshape(rows, n_st, 2, HEAD),
        ],
        axis=2,
    ).reshape(rows, -1)
    weight = jnp.concatenate([p[:, split:] for p in parts])
    weight = lax.all_gather(weight, "st", axis=1, tiled=True)
    weight = by_core(
        weight.reshape(chips, 1, depth, -1), to_core(weight).reshape(chips, 1, depth, -1), 1
    )
    order = jnp.zeros((chips,), jnp.int32).at[sources].set(jnp.arange(chips, dtype=jnp.int32))
    attended = lax.dot_general(
        heads,
        weight[order].reshape(width, -1),
        (((1,), (1,)), ((), ())),
        preferred_element_type=jnp.float32,
    ).astype(jnp.bfloat16)
    return attended.reshape(1, rows, width)


def solution(mesh):
    return jax.shard_map(
        functools.partial(shards, mesh.shape["st"], mesh.shape["fsdp"]),
        mesh=mesh,
        in_specs=(P("fsdp", None, None), P("fsdp", "st", None), P("fsdp", "st"), P()),
        out_specs=P("fsdp", "st", None),
        check_vma=False,
    )
```

```python
import functools
import math

import jax
import jax.numpy as jnp
from jax import lax
from jax.experimental import pallas as pl
from jax.experimental.pallas import tpu as pltpu
from jax.sharding import PartitionSpec as P

HEAD = 128
HS_DEV = 2
SCALE = 1.0 / math.sqrt(HEAD)
MIB = 1024 * 1024
LEADS = 5_000_000_000
PACKS = 1_000_000_000


def kernel_call(body, out_shape, args, flops, name, whole=(), scratch=(), limit=16 * MIB, out_space=pltpu.VMEM):
    bytes_moved = sum(a.size * a.dtype.itemsize for a in args)

    def space(i, a):
        if a.dtype == jnp.int32:
            return pltpu.SMEM
        return pltpu.VMEM if i in whole else pl.ANY

    return pl.pallas_call(
        body,
        out_shape=out_shape,
        in_specs=[pl.BlockSpec(memory_space=space(i, a)) for i, a in enumerate(args)],
        out_specs=pl.BlockSpec(memory_space=out_space),
        scratch_shapes=list(scratch),
        compiler_params=pltpu.CompilerParams(vmem_limit_bytes=limit),
        cost_estimate=pl.CostEstimate(flops=flops, bytes_accessed=bytes_moved, transcendentals=0),
        name=name,
    )(*args)


def weight_copies(depth, meta_ref, piece_refs, weight, sems):
    core = meta_ref[0]
    columns = weight.shape[1]
    slot, first = 0, 0
    copies = []
    for ref in piece_refs:
        rows = min(depth, ref.shape[0])
        for start in range(0, ref.shape[0], rows):
            chip = meta_ref[2 + slot]
            for k in range(2):
                at = (chip * 2 + (core if k == 0 else 1 - core)) * depth + first
                copies.append(
                    pltpu.make_async_copy(
                        ref.at[pl.ds(start, rows), pl.ds(k * columns, columns)],
                        weight.at[pl.ds(pl.multiple_of(at, 16), rows), :],
                        sems.at[len(copies)],
                    )
                )
            first += rows
            if first == depth:
                slot, first = slot + 1, 0
    return copies


def load_all(depth, meta_ref, own_ref, other_ref, piece_refs, weight, frames, sems):
    copies = weight_copies(depth, meta_ref, piece_refs, weight, sems)
    copies.append(pltpu.make_async_copy(own_ref, frames.at[0], sems.at[len(copies)]))
    last = pltpu.make_async_copy(other_ref, frames.at[1], sems.at[len(copies)])
    for copy in copies:
        copy.start()
    last.start()
    for copy in copies:
        copy.wait()
    return last


def load_scratch(copies, patches, width):
    return [
        pltpu.VMEM((width, 3 * HEAD), jnp.bfloat16),
        pltpu.VMEM((2, patches, width), jnp.bfloat16),
        pltpu.SemaphoreType.DMA((copies + 2,)),
    ]


def most_body(depth, meta_ref, own_ref, other_ref, *refs, copied=False):
    if copied:
        *piece_refs, out_ref, weight, frames, sems, sums, out_sems = refs
    else:
        *piece_refs, out_ref, weight, frames, sems = refs
        sums = out_ref
    for slot in range(len(piece_refs), weight.shape[0] // (2 * depth)):
        missing = meta_ref[2 + slot] * 2 * depth
        weight[pl.ds(pl.multiple_of(missing, 16), 2 * depth), :] = jnp.zeros(
            (2 * depth, weight.shape[1]), weight.dtype
        )
    last = load_all(depth, meta_ref, own_ref, other_ref, piece_refs, weight, frames, sems)
    patches = own_ref.shape[0]
    half = patches // 2
    copies = []
    for frame in range(2):
        if frame == 1:
            last.wait()
        for first in range(0, patches, half):
            here = slice(frame * patches + first, frame * patches + first + half)
            sums[here, :] = jnp.dot(
                frames[frame, first : first + half, :],
                weight[...],
                preferred_element_type=jnp.float32,
            )
            if copied:
                copies.append(
                    pltpu.make_async_copy(
                        sums.at[here, :], out_ref.at[here, :], out_sems.at[len(copies)]
                    )
                )
                copies[-1].start()
    for copy in copies:
        copy.wait()


def add_rest(
    depth, chips, meta_ref, own_ref, other_ref, most_ref, piece_refs, weight, frames, sems, fetch=None
):
    fetched = []
    if fetch is not None:
        most, fetch_sem = fetch
        fetched.append(pltpu.make_async_copy(most_ref, most, fetch_sem))
        most_ref = most
    patches = own_ref.shape[0]
    late = len(piece_refs)
    copies = [[], []]
    for k, ref in enumerate((own_ref, other_ref)):
        if ref.shape[1] == frames.shape[2]:
            copies[k].append(pltpu.make_async_copy(ref, frames.at[k], sems.at[k, 0]))
            continue
        for i in range(late):
            at = meta_ref[2 + chips - late + i] * 2 * depth
            copies[k].append(
                pltpu.make_async_copy(
                    ref.at[:, pl.ds(pl.multiple_of(at, 2 * depth), 2 * depth)],
                    frames.at[k, :, pl.ds(i * 2 * depth, 2 * depth)],
                    sems.at[k, i],
                )
            )
    for copy in fetched + copies[0] + copies[1]:
        copy.start()
    core = meta_ref[0]
    columns = weight.shape[1]
    for i, piece_ref in enumerate(piece_refs):
        for k in range(2):
            at = (2 * i + (core if k == 0 else 1 - core)) * depth
            weight[pl.ds(pl.multiple_of(at, 16), depth), :] = piece_ref[
                :, k * columns : (k + 1) * columns
            ]
    for copy in fetched:
        copy.wait()
    half = patches // 2
    for frame in range(2):
        for copy in copies[frame]:
            copy.wait()
        for first in range(0, patches, half):
            here = slice(frame * patches + first, frame * patches + first + half)
            result = most_ref[here, :] + jnp.dot(
                frames[frame, first : first + half, :],
                weight[...],
                preferred_element_type=jnp.float32,
            )
            yield frame, first, result.astype(jnp.bfloat16)


def rest_body(depth, chips, n_st, direct, late, meta_ref, own_ref, other_ref, most_ref, *refs):
    piece_refs, (out_ref, *scratch) = refs[:late], refs[late:]
    patches = own_ref.shape[0]
    part = patches // (n_st * chips)
    for frame, first, result in add_rest(
        depth, chips, meta_ref, own_ref, other_ref, most_ref, piece_refs, *scratch
    ):
        rows = result.shape[0]
        if not direct:
            out_ref[frame * patches + first : frame * patches + first + rows, :] = result
            continue
        for at in range(first, first + rows, part):
            block = at // part
            out_ref[block % chips, frame, block // chips] = result[at - first : at - first + part]


def spatial_body(depth, chips, n_st, late, meta_ref, own_ref, other_ref, most_ref, *refs):
    piece_refs, (out_ref, *scratch, packed, most, fetch_sem) = refs[:late], refs[late:]
    patches = own_ref.shape[0]
    part = patches // n_st
    for frame, first, result in add_rest(
        depth, chips, meta_ref, own_ref, other_ref, most_ref, piece_refs, *scratch, (most, fetch_sem)
    ):
        packed[first : first + result.shape[0], :] = result
        if first + result.shape[0] < patches:
            continue
        for group in range(n_st):
            rows = slice(group * part, (group + 1) * part)
            scores = lax.dot_general(
                packed[rows, :HEAD],
                packed[:, HEAD : 2 * HEAD],
                (((1,), (1,)), ((), ())),
                preferred_element_type=jnp.float32,
            )
            scores = scores * SCALE
            expo = jnp.exp(scores - jnp.max(scores, axis=-1, keepdims=True))
            total = jnp.sum(expo, axis=-1, keepdims=True)
            result = jnp.dot(
                expo.astype(jnp.bfloat16),
                packed[:, 2 * HEAD :],
                preferred_element_type=jnp.float32,
            )
            result = (result / total).astype(jnp.bfloat16)
            place = (group + meta_ref[1]) % 2 if n_st == 2 else group
            out_ref[place, frame] = result


def temporal_body(tile, meta_ref, qkv_ref, out_ref):
    frames, rows = qkv_ref.shape[0], qkv_ref.shape[1]
    part = out_ref.shape[2]
    flip = meta_ref[frames]
    size = frames * tile
    row_at = lax.broadcasted_iota(jnp.int32, (size, size), 0)
    col_at = lax.broadcasted_iota(jnp.int32, (size, size), 1)
    row_seg = jnp.zeros((size, 1), jnp.int32)
    col_seg = jnp.zeros((1, size), jnp.int32)
    row_frame = lax.broadcasted_iota(jnp.int32, (size, 1), 0) // tile
    col_frame = lax.broadcasted_iota(jnp.int32, (1, size), 1) // tile
    for frame in range(frames):
        clip = meta_ref[frame]
        row_seg = jnp.where(row_frame == frame, clip, row_seg)
        col_seg = jnp.where(col_frame == frame, clip, col_seg)
    keep = (row_at % tile == col_at % tile) & (row_seg == col_seg)
    for start in range(0, rows, tile):
        block = qkv_ref[:, start : start + tile, :].reshape(size, 3 * HEAD)
        scores = lax.dot_general(
            block[:, :HEAD],
            block[:, HEAD : 2 * HEAD],
            (((1,), (1,)), ((), ())),
            preferred_element_type=jnp.float32,
        )
        scores = jnp.where(keep, scores * SCALE, jnp.float32(-1e30))
        expo = jnp.exp(scores - jnp.max(scores, axis=-1, keepdims=True))
        total = jnp.sum(expo, axis=-1, keepdims=True)
        result = jnp.dot(
            expo.astype(jnp.bfloat16), block[:, 2 * HEAD :], preferred_element_type=jnp.float32
        )
        result = (result / total).astype(jnp.bfloat16).reshape(frames, tile, HEAD)
        for pair in range(frames // 2):
            for k in range(2):
                at = 2 * pair + (flip if k == 0 else 1 - flip)
                if part % tile:
                    out_ref[0, at, start : start + tile, :] = result[2 * pair + k]
                else:
                    low = start % part
                    out_ref[start // part, at, low : low + tile, :] = result[2 * pair + k]


def pack_body(split, *refs):
    *piece_refs, out_ref, sems = refs
    copies = []
    for i, ref in enumerate(piece_refs):
        rows, columns = ref.shape
        copies.append(
            pltpu.make_async_copy(
                ref.at[:, pl.ds(split, columns - split)],
                out_ref.at[i],
                sems.at[i],
            )
        )
    for copy in copies:
        copy.start()
    for copy in copies:
        copy.wait()


def order_body(received_ref, out_ref):
    n_st, chips, _, part, _ = received_ref.shape
    for group in range(n_st):
        for chip in range(chips):
            for k in range(2):
                out_ref[
                    group, chip * part : (chip + 1) * part, k * HEAD : (k + 1) * HEAD
                ] = received_ref[group, chip, k]


def out_body(
    depth, count, meta_ref, mine_ref, peer_ref, core_ref, far_ref, temporal_ref, *refs
):
    *weight_refs, out_ref, heads, weight, sems = refs
    core, st = meta_ref[0], meta_ref[1]
    n_st, chips = temporal_ref.shape[0], out_ref.shape[1] // (2 * depth)
    copies = [[] for _ in range(chips)]
    slot = 0
    for i in range(count):
        slots = weight_refs[i].shape[0]
        for kind in range(4):
            group = st if kind < 2 else 1 - st
            side = core if kind % 2 == 0 else 1 - core
            copies[slot].append(
                pltpu.make_async_copy(
                    weight_refs[kind * count + i],
                    weight.at[group, pl.ds(slot, slots), side],
                    sems.at[i, kind],
                )
            )
        slot += slots
    for copy in sum(copies, []):
        copy.start()
    mine, far = pl.multiple_of(core * HEAD, HEAD), pl.multiple_of((1 - core) * HEAD, HEAD)
    heads[st, :, pl.ds(mine, HEAD)] = mine_ref[...]
    heads[1 - st, :, pl.ds(mine, HEAD)] = peer_ref[...]
    heads[st, :, pl.ds(far, HEAD)] = core_ref[...]
    heads[1 - st, :, pl.ds(far, HEAD)] = far_ref[...]
    if len(temporal_ref.shape) == 3:
        heads[:, :, HS_DEV * HEAD :] = temporal_ref[...]
    else:
        part = temporal_ref.shape[3]
        for group in range(n_st):
            for chip in range(chips):
                for k in range(2):
                    heads[
                        group,
                        chip * part : (chip + 1) * part,
                        (HS_DEV + k) * HEAD : (HS_DEV + k + 1) * HEAD,
                    ] = temporal_ref[group, chip, k]
    chip_width = 2 * depth
    for slot in range(chips):
        for copy in copies[slot]:
            copy.wait()
        total = 0.0
        for group in range(n_st):
            total += lax.dot_general(
                heads[group],
                weight[group, slot].reshape(chip_width, -1),
                (((1,), (1,)), ((), ())),
                preferred_element_type=jnp.float32,
            )
        at = pl.multiple_of(meta_ref[2 + slot] * chip_width, chip_width)
        out_ref[:, pl.ds(at, chip_width)] = total.astype(jnp.bfloat16)


def shards(n_st, n_fsdp, normed, qkv_weight, out_weight, segment_ids):
    patches, width = normed.shape[1], normed.shape[2]
    frames = n_fsdp
    depth = qkv_weight.shape[0]
    chips = n_fsdp // 2
    part = patches // (n_st * chips)
    rows = patches // n_st
    direct = part % 16 == 0
    ring = list(range(0, chips, 2)) + list(range(chips - 1, 0, -2))
    place = [ring.index(chip) for chip in range(chips)]
    me = lax.axis_index("fsdp")
    st = lax.axis_index("st")
    chip, core = me // 2, me % 2
    spot = jnp.array(place, jnp.int32)[chip]

    swap = [(i, i ^ 1) for i in range(n_fsdp)]
    forward = [
        (2 * ring[i] + c, 2 * ring[(i + 1) % chips] + c) for i in range(chips) for c in range(2)
    ]
    backward = [(b, a) for a, b in forward]

    def to_core(x):
        return lax.ppermute(x, "fsdp", swap)

    def to_peer(x):
        return lax.ppermute(x, "st", [(0, 1), (1, 0)])

    def ring_gather(piece):
        pieces = [piece]
        ahead = behind = piece
        for _ in range(1, chips // 2):
            gate = yield pieces, ahead
            if gate is not None:
                ahead, behind, _ = lax.optimization_barrier((ahead, behind, gate))
            ahead = lax.ppermute(ahead, "fsdp", forward)
            behind = lax.ppermute(behind, "fsdp", backward)
            pieces = pieces + [ahead, behind]
        gate = yield pieces, ahead
        if gate is not None:
            ahead, behind, _ = lax.optimization_barrier((ahead, behind, gate))
        sent = jnp.where(core == 0, ahead, behind)
        gate = yield pieces, sent
        if gate is not None:
            sent, _ = lax.optimization_barrier((sent, gate))
        both = [edge for edge in forward if edge[0] % 2 == 0]
        both += [edge for edge in backward if edge[0] % 2 == 1]
        yield pieces + [lax.ppermute(sent, "fsdp", both)], None

    def run(ring, steps):
        for _ in range(steps):
            state = next(ring)
        return state

    offsets = [0]
    for d in range(1, chips // 2):
        offsets += [chips - d, d]
    offsets.append(chips // 2)
    sources = jnp.array(ring, jnp.int32)[(spot + jnp.array(offsets, jnp.int32)) % chips]
    here = jnp.stack([core, st])
    ring_meta = jnp.concatenate([here, sources]).astype(jnp.int32)

    by_head = qkv_weight.transpose(1, 0, 2)

    def take_head(heads):
        mine = lax.dynamic_index_in_dim(heads, core, 0, keepdims=False)
        other = lax.dynamic_index_in_dim(heads, 1 - core, 0, keepdims=False)
        return jnp.concatenate([mine, to_core(other)], axis=1)

    temporal_piece = take_head(lax.optimization_barrier(by_head[HS_DEV:]))
    own = normed.reshape(patches, width)

    temporal_ring = ring_gather(temporal_piece)
    second_pieces, _ = run(temporal_ring, 3)
    run(temporal_ring, chips // 2 - 2)
    pieces, _ = next(temporal_ring)
    own, later_head, _ = lax.optimization_barrier((own, by_head[:HS_DEV], temporal_piece))
    other = to_core(own)
    spatial_piece = take_head(later_head)
    split = spatial_piece.shape[1]
    both_ring = ring_gather(jnp.concatenate([spatial_piece, out_weight], axis=1))
    next(both_ring)
    both_ring.send(second_pieces[-1])
    temporal_late, spatial_late = 1, 3
    head_flops = 4 * patches * width * 3 * HEAD
    shape = (chips, 2, n_st, part, 3 * HEAD) if direct else (2 * patches, 3 * HEAD)
    most = kernel_call(
        functools.partial(most_body, depth),
        jax.ShapeDtypeStruct((2 * patches, 3 * HEAD), jnp.float32),
        [ring_meta, own, other, *pieces[: chips - temporal_late]],
        head_flops,
        "temporal_projection",
        scratch=load_scratch(2 * chips, patches, width),
    )

    def shares(late):
        if 2 * depth % 128 == 0:
            return own, other
        return [
            jnp.concatenate(
                [
                    lax.dynamic_slice_in_dim(x, sources[chips - i] * 2 * depth, 2 * depth, 1)
                    for i in range(late, 0, -1)
                ],
                axis=1,
            )
            for x in (own, other)
        ]

    def rest_scratch(late):
        return [
            pltpu.VMEM((late * 2 * depth, 3 * HEAD), jnp.bfloat16),
            pltpu.VMEM((2, patches, late * 2 * depth), jnp.bfloat16),
            pltpu.SemaphoreType.DMA((2, late)),
        ]

    temporal = kernel_call(
        functools.partial(rest_body, depth, chips, n_st, direct, temporal_late),
        jax.ShapeDtypeStruct(shape, jnp.bfloat16),
        [ring_meta, *shares(temporal_late), most, *pieces[chips - temporal_late :]],
        head_flops // chips,
        "temporal_projection_rest",
        whole=range(3, 4 + temporal_late),
        scratch=rest_scratch(temporal_late),
    )
    if not direct:
        temporal = temporal.reshape(2, n_st, chips, part, 3 * HEAD).transpose(2, 0, 1, 3, 4)
    second_parts, _ = both_ring.send(most)
    if chips > 8:
        second_parts, _ = run(both_ring, chips // 2 - 4)
    spatial_most = kernel_call(
        functools.partial(most_body, depth, copied=True),
        jax.ShapeDtypeStruct((2 * patches, 3 * HEAD), jnp.float32),
        [ring_meta, own, other, *second_parts[: chips - spatial_late]],
        0,
        "spatial_projection",
        scratch=[
            *load_scratch(2 * chips, patches, width),
            pltpu.VMEM((2 * patches, 3 * HEAD), jnp.float32),
            pltpu.SemaphoreType.DMA((4,)),
        ],
        out_space=pl.ANY,
    )
    third_parts, _ = both_ring.send(None)
    same_core = [[2 * i + c for i in range(chips)] for c in range(2)]
    temporal = lax.all_to_all(
        temporal,
        "fsdp",
        split_axis=0,
        concat_axis=0,
        tiled=True,
        axis_index_groups=same_core,
    ).reshape(frames, n_st * part, 3 * HEAD)
    pairs = segment_ids.reshape(chips, 2)
    pairs = jnp.where(core == 0, pairs, pairs[:, ::-1]).reshape(frames)
    clips = jnp.concatenate([pairs, core.reshape(1)]).astype(jnp.int32)
    temporal, _ = lax.optimization_barrier((temporal, third_parts[-1]))
    tile = min(n_st * part, max(16, 256 // frames))
    if part % tile == 0:
        shape = (n_st, frames, part, HEAD)
    else:
        shape = (1, frames, n_st * part, HEAD)
    result = attention = kernel_call(
        functools.partial(temporal_body, tile),
        jax.ShapeDtypeStruct(shape, jnp.bfloat16),
        [clips, temporal],
        LEADS,
        "temporal_attention",
        whole=(1,),
    )
    if part % tile:
        result = result.reshape(frames, n_st, part, HEAD).transpose(1, 0, 2, 3)
    result = lax.all_to_all(
        result.reshape(n_st * frames, part, HEAD),
        ("st", "fsdp"),
        split_axis=0,
        concat_axis=0,
        tiled=True,
    )
    temporal_heads = result.reshape(n_st, chips, 2, part, HEAD)

    def pack(group):
        return kernel_call(
            functools.partial(pack_body, split),
            jax.ShapeDtypeStruct((len(group), depth, out_weight.shape[1]), jnp.bfloat16),
            group,
            PACKS,
            "pack_out_weight",
            scratch=[pltpu.SemaphoreType.DMA((len(group),))],
            limit=60 * MIB,
        )

    early = n_st == 2 and direct
    parts = second_parts
    if early:
        kinds = [pack(parts[:3]), pack(parts[3:5])]
        peers = [to_peer(k) for k in kinds]
    both_ring.send(spatial_most)
    parts, _ = both_ring.send((attention, *peers) if early else attention)
    spatial = kernel_call(
        functools.partial(spatial_body, depth, chips, n_st, spatial_late),
        jax.ShapeDtypeStruct((n_st, 2, rows, HEAD), jnp.bfloat16),
        [ring_meta, *shares(spatial_late), spatial_most, *parts[chips - spatial_late :]],
        0,
        "spatial_heads",
        whole=range(4, 4 + spatial_late),
        scratch=[
            *rest_scratch(spatial_late),
            pltpu.VMEM((patches, 3 * HEAD), jnp.bfloat16),
            pltpu.VMEM((2 * patches, 3 * HEAD), jnp.float32),
            pltpu.SemaphoreType.DMA,
        ],
    )

    if early:
        temporal_heads = kernel_call(
            order_body,
            jax.ShapeDtypeStruct((n_st, rows, 2 * HEAD), jnp.bfloat16),
            [temporal_heads],
            LEADS,
            "temporal_heads",
            whole=(0,),
        )
        across = [(i, (i ^ 1 ^ n_fsdp)) for i in range(n_st * n_fsdp)]
        received = [
            to_peer(spatial[1, 0]),
            to_core(spatial[0, 1]),
            lax.ppermute(spatial[1, 1], ("st", "fsdp"), across),
        ]

        kinds += [pack(parts[at : at + 2]) for at in range(5, chips, 2)]
        peers += [to_peer(k) for k in kinds[2:]]
        count = len(kinds)
        kinds += [to_core(k) for k in kinds] + peers
        peers = lax.optimization_barrier((*peers, spatial))[:-1]
        kinds += [to_core(k) for k in peers]
        attended = kernel_call(
            functools.partial(out_body, depth, count),
            jax.ShapeDtypeStruct((rows, width), jnp.bfloat16),
            [ring_meta, spatial[0, 0], *received, temporal_heads, *kinds],
            4 * rows * width * out_weight.shape[1],
            "out_projection",
            whole=(1, 2, 3, 4, 5),
            scratch=[
                pltpu.VMEM((n_st, rows, out_weight.shape[1]), jnp.bfloat16),
                pltpu.VMEM((n_st, chips, 2, depth, out_weight.shape[1]), jnp.bfloat16),
                pltpu.SemaphoreType.DMA((count, 4)),
            ],
            limit=60 * MIB,
        )
        return attended.reshape(1, rows, width)

    def by_core(mine, other, axis):
        return jnp.where(
            core == 0,
            jnp.concatenate([mine, other], axis=axis),
            jnp.concatenate([other, mine], axis=axis),
        )

    if n_st == 2:
        spatial = jnp.where(st == 0, spatial, spatial[::-1])
    spatial = lax.all_to_all(spatial, "st", split_axis=0, concat_axis=0, tiled=True)
    spatial = by_core(spatial[:, 0, :, None], to_core(spatial[:, 1])[:, :, None], 2)
    heads = jnp.concatenate(
        [
            spatial.transpose(1, 0, 2, 3),
            temporal_heads.transpose(1, 3, 0, 2, 4).reshape(rows, n_st, 2, HEAD),
        ],
        axis=2,
    ).reshape(rows, -1)
    weight = jnp.concatenate([p[:, split:] for p in parts])
    weight = lax.all_gather(weight, "st", axis=1, tiled=True)
    weight = by_core(
        weight.reshape(chips, 1, depth, -1), to_core(weight).reshape(chips, 1, depth, -1), 1
    )
    order = jnp.zeros((chips,), jnp.int32).at[sources].set(jnp.arange(chips, dtype=jnp.int32))
    attended = lax.dot_general(
        heads,
        weight[order].reshape(width, -1),
        (((1,), (1,)), ((), ())),
        preferred_element_type=jnp.float32,
    ).astype(jnp.bfloat16)
    return attended.reshape(1, rows, width)


def solution(mesh):
    return jax.shard_map(
        functools.partial(shards, mesh.shape["st"], mesh.shape["fsdp"]),
        mesh=mesh,
        in_specs=(P("fsdp", None, None), P("fsdp", "st", None), P("fsdp", "st"), P()),
        out_specs=P("fsdp", "st", None),
        check_vma=False,
    )
```

```python
import functools
import math

import jax
import jax.numpy as jnp
from jax import lax
from jax.experimental import pallas as pl
from jax.experimental.pallas import tpu as pltpu
from jax.sharding import PartitionSpec as P

HEAD = 128
HS_DEV = 2
SCALE = 1.0 / math.sqrt(HEAD)
SCALE_LOG2 = SCALE * math.log2(math.e)
MIB = 1024 * 1024
LEADS = 5_000_000_000
PACKS = 1_000_000_000


def kernel_call(body, out_shape, args, flops, name, whole=(), scratch=(), limit=16 * MIB, out_space=pltpu.VMEM):
    bytes_moved = sum(a.size * a.dtype.itemsize for a in args)

    def space(i, a):
        if a.dtype == jnp.int32:
            return pltpu.SMEM
        return pltpu.VMEM if i in whole else pl.ANY

    return pl.pallas_call(
        body,
        out_shape=out_shape,
        in_specs=[pl.BlockSpec(memory_space=space(i, a)) for i, a in enumerate(args)],
        out_specs=pl.BlockSpec(memory_space=out_space),
        scratch_shapes=list(scratch),
        compiler_params=pltpu.CompilerParams(vmem_limit_bytes=limit),
        cost_estimate=pl.CostEstimate(flops=flops, bytes_accessed=bytes_moved, transcendentals=0),
        name=name,
    )(*args)


def weight_copies(depth, meta_ref, piece_refs, weight, sems):
    core = meta_ref[0]
    columns = weight.shape[1]
    slot, first = 0, 0
    copies = []
    for ref in piece_refs:
        rows = min(depth, ref.shape[0])
        for start in range(0, ref.shape[0], rows):
            chip = meta_ref[2 + slot]
            for k in range(2):
                at = (chip * 2 + (core if k == 0 else 1 - core)) * depth + first
                copies.append(
                    pltpu.make_async_copy(
                        ref.at[pl.ds(start, rows), pl.ds(k * columns, columns)],
                        weight.at[pl.ds(pl.multiple_of(at, 16), rows), :],
                        sems.at[len(copies)],
                    )
                )
            first += rows
            if first == depth:
                slot, first = slot + 1, 0
    return copies


def load_all(depth, meta_ref, own_ref, other_ref, piece_refs, weight, frames, sems):
    copies = weight_copies(depth, meta_ref, piece_refs, weight, sems)
    copies.append(pltpu.make_async_copy(own_ref, frames.at[0], sems.at[len(copies)]))
    last = pltpu.make_async_copy(other_ref, frames.at[1], sems.at[len(copies)])
    for copy in copies:
        copy.start()
    last.start()
    for copy in copies:
        copy.wait()
    return last


def load_scratch(copies, patches, width):
    return [
        pltpu.VMEM((width, 3 * HEAD), jnp.bfloat16),
        pltpu.VMEM((2, patches, width), jnp.bfloat16),
        pltpu.SemaphoreType.DMA((copies + 2,)),
    ]


def most_body(depth, meta_ref, own_ref, other_ref, *refs, copied=False):
    if copied:
        *piece_refs, out_ref, weight, frames, sems, sums, out_sems = refs
    else:
        *piece_refs, out_ref, weight, frames, sems = refs
        sums = out_ref
    for slot in range(len(piece_refs), weight.shape[0] // (2 * depth)):
        missing = meta_ref[2 + slot] * 2 * depth
        weight[pl.ds(pl.multiple_of(missing, 16), 2 * depth), :] = jnp.zeros(
            (2 * depth, weight.shape[1]), weight.dtype
        )
    last = load_all(depth, meta_ref, own_ref, other_ref, piece_refs, weight, frames, sems)
    patches = own_ref.shape[0]
    half = patches // 2
    copies = []
    for frame in range(2):
        if frame == 1:
            last.wait()
        for first in range(0, patches, half):
            here = slice(frame * patches + first, frame * patches + first + half)
            sums[here, :] = jnp.dot(
                frames[frame, first : first + half, :],
                weight[...],
                preferred_element_type=jnp.float32,
            )
            if copied:
                copies.append(
                    pltpu.make_async_copy(
                        sums.at[here, :], out_ref.at[here, :], out_sems.at[len(copies)]
                    )
                )
                copies[-1].start()
    for copy in copies:
        copy.wait()


def add_rest(
    depth, chips, meta_ref, own_ref, other_ref, most_ref, piece_refs, weight, frames, sems, fetch=None
):
    fetched = []
    if fetch is not None:
        most, fetch_sem = fetch
        fetched.append(pltpu.make_async_copy(most_ref, most, fetch_sem))
        most_ref = most
    patches = own_ref.shape[0]
    late = len(piece_refs)
    copies = [[], []]
    for k, ref in enumerate((own_ref, other_ref)):
        if ref.shape[1] == frames.shape[2]:
            copies[k].append(pltpu.make_async_copy(ref, frames.at[k], sems.at[k, 0]))
            continue
        for i in range(late):
            at = meta_ref[2 + chips - late + i] * 2 * depth
            copies[k].append(
                pltpu.make_async_copy(
                    ref.at[:, pl.ds(pl.multiple_of(at, 2 * depth), 2 * depth)],
                    frames.at[k, :, pl.ds(i * 2 * depth, 2 * depth)],
                    sems.at[k, i],
                )
            )
    for copy in fetched + copies[0] + copies[1]:
        copy.start()
    core = meta_ref[0]
    columns = weight.shape[1]
    for i, piece_ref in enumerate(piece_refs):
        for k in range(2):
            at = (2 * i + (core if k == 0 else 1 - core)) * depth
            weight[pl.ds(pl.multiple_of(at, 16), depth), :] = piece_ref[
                :, k * columns : (k + 1) * columns
            ]
    for copy in fetched:
        copy.wait()
    half = patches // 2
    for frame in range(2):
        for copy in copies[frame]:
            copy.wait()
        for first in range(0, patches, half):
            here = slice(frame * patches + first, frame * patches + first + half)
            result = most_ref[here, :] + jnp.dot(
                frames[frame, first : first + half, :],
                weight[...],
                preferred_element_type=jnp.float32,
            )
            yield frame, first, result.astype(jnp.bfloat16)


def rest_body(depth, chips, n_st, direct, late, meta_ref, own_ref, other_ref, most_ref, *refs):
    piece_refs, (out_ref, *scratch) = refs[:late], refs[late:]
    patches = own_ref.shape[0]
    part = patches // (n_st * chips)
    for frame, first, result in add_rest(
        depth, chips, meta_ref, own_ref, other_ref, most_ref, piece_refs, *scratch
    ):
        rows = result.shape[0]
        if not direct:
            out_ref[frame * patches + first : frame * patches + first + rows, :] = result
            continue
        for at in range(first, first + rows, part):
            block = at // part
            out_ref[block % chips, frame, block // chips] = result[at - first : at - first + part]


def spatial_body(depth, chips, n_st, late, meta_ref, own_ref, other_ref, most_ref, *refs):
    piece_refs, (out_ref, *scratch, packed, most, fetch_sem) = refs[:late], refs[late:]
    patches = own_ref.shape[0]
    part = patches // n_st
    for frame, first, result in add_rest(
        depth, chips, meta_ref, own_ref, other_ref, most_ref, piece_refs, *scratch, (most, fetch_sem)
    ):
        packed[first : first + result.shape[0], :] = result
        if first + result.shape[0] < patches:
            continue
        for group in range(n_st):
            rows = slice(group * part, (group + 1) * part)
            scores = lax.dot_general(
                packed[rows, :HEAD],
                packed[:, HEAD : 2 * HEAD],
                (((1,), (1,)), ((), ())),
                preferred_element_type=jnp.float32,
            )
            expo = jnp.exp2((scores - jnp.max(scores, axis=-1, keepdims=True)) * SCALE_LOG2)
            total = jnp.sum(expo, axis=-1, keepdims=True)
            result = jnp.dot(
                expo.astype(jnp.bfloat16),
                packed[:, 2 * HEAD :],
                preferred_element_type=jnp.float32,
            )
            result = (result / total).astype(jnp.bfloat16)
            place = (group + meta_ref[1]) % 2 if n_st == 2 else group
            out_ref[place, frame] = result


def temporal_body(tile, meta_ref, qkv_ref, out_ref):
    frames, rows = qkv_ref.shape[0], qkv_ref.shape[1]
    part = out_ref.shape[2]
    flip = meta_ref[frames]
    size = frames * tile
    row_at = lax.broadcasted_iota(jnp.int32, (size, size), 0)
    col_at = lax.broadcasted_iota(jnp.int32, (size, size), 1)
    row_seg = jnp.zeros((size, 1), jnp.int32)
    col_seg = jnp.zeros((1, size), jnp.int32)
    row_frame = lax.broadcasted_iota(jnp.int32, (size, 1), 0) // tile
    col_frame = lax.broadcasted_iota(jnp.int32, (1, size), 1) // tile
    for frame in range(frames):
        clip = meta_ref[frame]
        row_seg = jnp.where(row_frame == frame, clip, row_seg)
        col_seg = jnp.where(col_frame == frame, clip, col_seg)
    keep = (row_at % tile == col_at % tile) & (row_seg == col_seg)
    for start in range(0, rows, tile):
        block = qkv_ref[:, start : start + tile, :].reshape(size, 3 * HEAD)
        scores = lax.dot_general(
            block[:, :HEAD],
            block[:, HEAD : 2 * HEAD],
            (((1,), (1,)), ((), ())),
            preferred_element_type=jnp.float32,
        )
        scores = jnp.where(keep, scores * SCALE, jnp.float32(-1e30))
        expo = jnp.exp(scores - jnp.max(scores, axis=-1, keepdims=True))
        total = jnp.sum(expo, axis=-1, keepdims=True)
        result = jnp.dot(
            expo.astype(jnp.bfloat16), block[:, 2 * HEAD :], preferred_element_type=jnp.float32
        )
        result = (result / total).astype(jnp.bfloat16).reshape(frames, tile, HEAD)
        for pair in range(frames // 2):
            for k in range(2):
                at = 2 * pair + (flip if k == 0 else 1 - flip)
                if part % tile:
                    out_ref[0, at, start : start + tile, :] = result[2 * pair + k]
                else:
                    low = start % part
                    out_ref[start // part, at, low : low + tile, :] = result[2 * pair + k]


def pack_body(split, *refs):
    *piece_refs, out_ref, sems = refs
    copies = []
    for i, ref in enumerate(piece_refs):
        rows, columns = ref.shape
        copies.append(
            pltpu.make_async_copy(
                ref.at[:, pl.ds(split, columns - split)],
                out_ref.at[i],
                sems.at[i],
            )
        )
    for copy in copies:
        copy.start()
    for copy in copies:
        copy.wait()


def order_body(received_ref, out_ref):
    n_st, chips, _, part, _ = received_ref.shape
    for group in range(n_st):
        for chip in range(chips):
            for k in range(2):
                out_ref[
                    group, chip * part : (chip + 1) * part, k * HEAD : (k + 1) * HEAD
                ] = received_ref[group, chip, k]


def out_body(
    depth, count, meta_ref, mine_ref, peer_ref, core_ref, far_ref, temporal_ref, *refs
):
    *weight_refs, out_ref, heads, weight, sems, result, out_sems = refs
    core, st = meta_ref[0], meta_ref[1]
    n_st, chips = temporal_ref.shape[0], out_ref.shape[1] // (2 * depth)
    copies = [[] for _ in range(chips)]
    slot = 0
    for i in range(count):
        slots = weight_refs[i].shape[0]
        for kind in range(4):
            group = st if kind < 2 else 1 - st
            side = core if kind % 2 == 0 else 1 - core
            copies[slot].append(
                pltpu.make_async_copy(
                    weight_refs[kind * count + i],
                    weight.at[group, pl.ds(slot, slots), side],
                    sems.at[i, kind],
                )
            )
        slot += slots
    for copy in sum(copies, []):
        copy.start()
    mine, far = pl.multiple_of(core * HEAD, HEAD), pl.multiple_of((1 - core) * HEAD, HEAD)
    heads[st, :, pl.ds(mine, HEAD)] = mine_ref[...]
    heads[1 - st, :, pl.ds(mine, HEAD)] = peer_ref[...]
    heads[st, :, pl.ds(far, HEAD)] = core_ref[...]
    heads[1 - st, :, pl.ds(far, HEAD)] = far_ref[...]
    if len(temporal_ref.shape) == 3:
        heads[:, :, HS_DEV * HEAD :] = temporal_ref[...]
    else:
        part = temporal_ref.shape[3]
        for group in range(n_st):
            for chip in range(chips):
                for k in range(2):
                    heads[
                        group,
                        chip * part : (chip + 1) * part,
                        (HS_DEV + k) * HEAD : (HS_DEV + k + 1) * HEAD,
                    ] = temporal_ref[group, chip, k]
    chip_width = 2 * depth
    out_copies = []
    for slot in range(chips):
        for copy in copies[slot]:
            copy.wait()
        total = 0.0
        for group in range(n_st):
            total += lax.dot_general(
                heads[group],
                weight[group, slot].reshape(chip_width, -1),
                (((1,), (1,)), ((), ())),
                preferred_element_type=jnp.float32,
            )
        at = pl.multiple_of(meta_ref[2 + slot] * chip_width, chip_width)
        result[slot] = total.astype(jnp.bfloat16)
        out_copies.append(
            pltpu.make_async_copy(
                result.at[slot], out_ref.at[:, pl.ds(at, chip_width)], out_sems.at[slot]
            )
        )
        out_copies[-1].start()
    for copy in out_copies:
        copy.wait()


def shards(n_st, n_fsdp, normed, qkv_weight, out_weight, segment_ids):
    patches, width = normed.shape[1], normed.shape[2]
    frames = n_fsdp
    depth = qkv_weight.shape[0]
    chips = n_fsdp // 2
    part = patches // (n_st * chips)
    rows = patches // n_st
    direct = part % 16 == 0
    ring = list(range(0, chips, 2)) + list(range(chips - 1, 0, -2))
    place = [ring.index(chip) for chip in range(chips)]
    me = lax.axis_index("fsdp")
    st = lax.axis_index("st")
    chip, core = me // 2, me % 2
    spot = jnp.array(place, jnp.int32)[chip]

    swap = [(i, i ^ 1) for i in range(n_fsdp)]
    forward = [
        (2 * ring[i] + c, 2 * ring[(i + 1) % chips] + c) for i in range(chips) for c in range(2)
    ]
    backward = [(b, a) for a, b in forward]

    def to_core(x):
        return lax.ppermute(x, "fsdp", swap)

    def to_peer(x):
        return lax.ppermute(x, "st", [(0, 1), (1, 0)])

    def ring_gather(piece):
        pieces = [piece]
        ahead = behind = piece
        for _ in range(1, chips // 2):
            gate = yield pieces, ahead
            if gate is not None:
                ahead, behind, _ = lax.optimization_barrier((ahead, behind, gate))
            ahead = lax.ppermute(ahead, "fsdp", forward)
            behind = lax.ppermute(behind, "fsdp", backward)
            pieces = pieces + [ahead, behind]
        gate = yield pieces, ahead
        if gate is not None:
            ahead, behind, _ = lax.optimization_barrier((ahead, behind, gate))
        sent = jnp.where(core == 0, ahead, behind)
        gate = yield pieces, sent
        if gate is not None:
            sent, _ = lax.optimization_barrier((sent, gate))
        both = [edge for edge in forward if edge[0] % 2 == 0]
        both += [edge for edge in backward if edge[0] % 2 == 1]
        yield pieces + [lax.ppermute(sent, "fsdp", both)], None

    def run(ring, steps):
        for _ in range(steps):
            state = next(ring)
        return state

    offsets = [0]
    for d in range(1, chips // 2):
        offsets += [chips - d, d]
    offsets.append(chips // 2)
    sources = jnp.array(ring, jnp.int32)[(spot + jnp.array(offsets, jnp.int32)) % chips]
    here = jnp.stack([core, st])
    ring_meta = jnp.concatenate([here, sources]).astype(jnp.int32)

    by_head = qkv_weight.transpose(1, 0, 2)

    def take_head(heads):
        mine = lax.dynamic_index_in_dim(heads, core, 0, keepdims=False)
        other = lax.dynamic_index_in_dim(heads, 1 - core, 0, keepdims=False)
        return jnp.concatenate([mine, to_core(other)], axis=1)

    temporal_piece = take_head(lax.optimization_barrier(by_head[HS_DEV:]))
    own = normed.reshape(patches, width)

    temporal_ring = ring_gather(temporal_piece)
    second_pieces, _ = run(temporal_ring, 3)
    run(temporal_ring, chips // 2 - 2)
    pieces, _ = next(temporal_ring)
    own, later_head, _ = lax.optimization_barrier((own, by_head[:HS_DEV], temporal_piece))
    other = to_core(own)
    spatial_piece = take_head(later_head)
    split = spatial_piece.shape[1]
    both_ring = ring_gather(jnp.concatenate([spatial_piece, out_weight], axis=1))
    next(both_ring)
    both_ring.send(second_pieces[-1])
    temporal_late, spatial_late = 1, 3
    head_flops = 4 * patches * width * 3 * HEAD
    shape = (chips, 2, n_st, part, 3 * HEAD) if direct else (2 * patches, 3 * HEAD)
    most = kernel_call(
        functools.partial(most_body, depth),
        jax.ShapeDtypeStruct((2 * patches, 3 * HEAD), jnp.float32),
        [ring_meta, own, other, *pieces[: chips - temporal_late]],
        head_flops,
        "temporal_projection",
        scratch=load_scratch(2 * chips, patches, width),
    )

    def shares(late):
        if 2 * depth % 128 == 0:
            return own, other
        return [
            jnp.concatenate(
                [
                    lax.dynamic_slice_in_dim(x, sources[chips - i] * 2 * depth, 2 * depth, 1)
                    for i in range(late, 0, -1)
                ],
                axis=1,
            )
            for x in (own, other)
        ]

    def rest_scratch(late):
        return [
            pltpu.VMEM((late * 2 * depth, 3 * HEAD), jnp.bfloat16),
            pltpu.VMEM((2, patches, late * 2 * depth), jnp.bfloat16),
            pltpu.SemaphoreType.DMA((2, late)),
        ]

    temporal = kernel_call(
        functools.partial(rest_body, depth, chips, n_st, direct, temporal_late),
        jax.ShapeDtypeStruct(shape, jnp.bfloat16),
        [ring_meta, *shares(temporal_late), most, *pieces[chips - temporal_late :]],
        head_flops // chips,
        "temporal_projection_rest",
        whole=range(3, 4 + temporal_late),
        scratch=rest_scratch(temporal_late),
    )
    if not direct:
        temporal = temporal.reshape(2, n_st, chips, part, 3 * HEAD).transpose(2, 0, 1, 3, 4)
    second_parts, _ = both_ring.send(most)
    if chips > 8:
        second_parts, _ = run(both_ring, chips // 2 - 4)
    spatial_most = kernel_call(
        functools.partial(most_body, depth, copied=True),
        jax.ShapeDtypeStruct((2 * patches, 3 * HEAD), jnp.float32),
        [ring_meta, own, other, *second_parts[: chips - spatial_late]],
        0,
        "spatial_projection",
        scratch=[
            *load_scratch(2 * chips, patches, width),
            pltpu.VMEM((2 * patches, 3 * HEAD), jnp.float32),
            pltpu.SemaphoreType.DMA((4,)),
        ],
        out_space=pl.ANY,
    )
    third_parts, _ = both_ring.send(None)
    same_core = [[2 * i + c for i in range(chips)] for c in range(2)]
    temporal = lax.all_to_all(
        temporal,
        "fsdp",
        split_axis=0,
        concat_axis=0,
        tiled=True,
        axis_index_groups=same_core,
    ).reshape(frames, n_st * part, 3 * HEAD)
    pairs = segment_ids.reshape(chips, 2)
    pairs = jnp.where(core == 0, pairs, pairs[:, ::-1]).reshape(frames)
    clips = jnp.concatenate([pairs, core.reshape(1)]).astype(jnp.int32)
    temporal, _ = lax.optimization_barrier((temporal, third_parts[-1]))
    tile = min(n_st * part, max(16, 256 // frames))
    if part % tile == 0:
        shape = (n_st, frames, part, HEAD)
    else:
        shape = (1, frames, n_st * part, HEAD)
    result = attention = kernel_call(
        functools.partial(temporal_body, tile),
        jax.ShapeDtypeStruct(shape, jnp.bfloat16),
        [clips, temporal],
        LEADS,
        "temporal_attention",
        whole=(1,),
    )
    if part % tile:
        result = result.reshape(frames, n_st, part, HEAD).transpose(1, 0, 2, 3)
    result = lax.all_to_all(
        result.reshape(n_st * frames, part, HEAD),
        ("st", "fsdp"),
        split_axis=0,
        concat_axis=0,
        tiled=True,
    )
    temporal_heads = result.reshape(n_st, chips, 2, part, HEAD)

    def pack(group):
        return kernel_call(
            functools.partial(pack_body, split),
            jax.ShapeDtypeStruct((len(group), depth, out_weight.shape[1]), jnp.bfloat16),
            group,
            PACKS,
            "pack_out_weight",
            scratch=[pltpu.SemaphoreType.DMA((len(group),))],
            limit=60 * MIB,
        )

    early = n_st == 2 and direct
    parts = second_parts
    if early:
        kinds = [pack(parts[:3]), pack(parts[3:5])]
        peers = [to_peer(k) for k in kinds]
    both_ring.send(spatial_most)
    parts, _ = both_ring.send((attention, *peers) if early else attention)
    spatial = kernel_call(
        functools.partial(spatial_body, depth, chips, n_st, spatial_late),
        jax.ShapeDtypeStruct((n_st, 2, rows, HEAD), jnp.bfloat16),
        [ring_meta, *shares(spatial_late), spatial_most, *parts[chips - spatial_late :]],
        0,
        "spatial_heads",
        whole=range(4, 4 + spatial_late),
        scratch=[
            *rest_scratch(spatial_late),
            pltpu.VMEM((patches, 3 * HEAD), jnp.bfloat16),
            pltpu.VMEM((2 * patches, 3 * HEAD), jnp.float32),
            pltpu.SemaphoreType.DMA,
        ],
    )

    if early:
        temporal_heads = kernel_call(
            order_body,
            jax.ShapeDtypeStruct((n_st, rows, 2 * HEAD), jnp.bfloat16),
            [temporal_heads],
            LEADS,
            "temporal_heads",
            whole=(0,),
        )
        across = [(i, (i ^ 1 ^ n_fsdp)) for i in range(n_st * n_fsdp)]
        received = [
            to_peer(spatial[1, 0]),
            to_core(spatial[0, 1]),
            lax.ppermute(spatial[1, 1], ("st", "fsdp"), across),
        ]

        kinds += [pack(parts[at : at + 2]) for at in range(5, chips, 2)]
        peers += [to_peer(k) for k in kinds[2:]]
        count = len(kinds)
        kinds += [to_core(k) for k in kinds] + peers
        peers = lax.optimization_barrier((*peers, spatial))[:-1]
        kinds += [to_core(k) for k in peers]
        attended = kernel_call(
            functools.partial(out_body, depth, count),
            jax.ShapeDtypeStruct((rows, width), jnp.bfloat16),
            [ring_meta, spatial[0, 0], *received, temporal_heads, *kinds],
            4 * rows * width * out_weight.shape[1],
            "out_projection",
            whole=(1, 2, 3, 4, 5),
            scratch=[
                pltpu.VMEM((n_st, rows, out_weight.shape[1]), jnp.bfloat16),
                pltpu.VMEM((n_st, chips, 2, depth, out_weight.shape[1]), jnp.bfloat16),
                pltpu.SemaphoreType.DMA((count, 4)),
                pltpu.VMEM((chips, rows, 2 * depth), jnp.bfloat16),
                pltpu.SemaphoreType.DMA((chips,)),
            ],
            limit=60 * MIB,
            out_space=pl.ANY,
        )
        return attended.reshape(1, rows, width)

    def by_core(mine, other, axis):
        return jnp.where(
            core == 0,
            jnp.concatenate([mine, other], axis=axis),
            jnp.concatenate([other, mine], axis=axis),
        )

    if n_st == 2:
        spatial = jnp.where(st == 0, spatial, spatial[::-1])
    spatial = lax.all_to_all(spatial, "st", split_axis=0, concat_axis=0, tiled=True)
    spatial = by_core(spatial[:, 0, :, None], to_core(spatial[:, 1])[:, :, None], 2)
    heads = jnp.concatenate(
        [
            spatial.transpose(1, 0, 2, 3),
            temporal_heads.transpose(1, 3, 0, 2, 4).reshape(rows, n_st, 2, HEAD),
        ],
        axis=2,
    ).reshape(rows, -1)
    weight = jnp.concatenate([p[:, split:] for p in parts])
    weight = lax.all_gather(weight, "st", axis=1, tiled=True)
    weight = by_core(
        weight.reshape(chips, 1, depth, -1), to_core(weight).reshape(chips, 1, depth, -1), 1
    )
    order = jnp.zeros((chips,), jnp.int32).at[sources].set(jnp.arange(chips, dtype=jnp.int32))
    attended = lax.dot_general(
        heads,
        weight[order].reshape(width, -1),
        (((1,), (1,)), ((), ())),
        preferred_element_type=jnp.float32,
    ).astype(jnp.bfloat16)
    return attended.reshape(1, rows, width)


def solution(mesh):
    return jax.shard_map(
        functools.partial(shards, mesh.shape["st"], mesh.shape["fsdp"]),
        mesh=mesh,
        in_specs=(P("fsdp", None, None), P("fsdp", "st", None), P("fsdp", "st"), P()),
        out_specs=P("fsdp", "st", None),
        check_vma=False,
    )
```
